128 devices in a mesh: gx: 16 (over z, y), gy: 8 (over x, core).
Axes of the slice: x: 4, y: 4, z: 4, core: 2. Of those that a mesh axis runs over, the one named last changes fastest.
Arguments:
- disp_start: float32 [3, 128, 32, 2048], P(None, 'gx', None, 'gy'), may hold values from -6 to 6
- load: float32 [3, 128, 32, 2048], P(None, 'gx', None, 'gy'), may hold values from -24 to 24
- modulus: float32 [128, 32, 2048], P('gx', None, 'gy'), may hold values from 0.5 to 2
- element_matrix: float32 [24, 24], replicated, may hold values from -0.08 to 1.2, as said below
- precond: float32 [9, 128, 32, 2048], P(None, 'gx', None, 'gy'), may hold values from -0.03 to 0.2
- approach: float32 [128], P('gx'), may hold values from 0.5 to 2.5
- contact: int32 [128, 32], P('gx', 'gy'), may hold values from 0 to 1, as said below
- owner: int32 [128, 32], P('gx', 'gy'), may hold values from 0 to 15, as said below
- slot: int32 [128, 32], P('gx', 'gy'), may hold values from 0 to 1, as said below
- influence: float32 [16, 8, 16, 2, 64, 64], P('gx', 'gy'), may hold values from -0.5 to 0.6
Outputs:
- displacement: float32 [3, 128, 32, 2048], P(None, 'gx', None, 'gy')
- pressure: float32 [128, 2048], P('gx', 'gy')
The draws below stay inside these ranges and needn't reach their ends.
Inputs may be any that keep to these rules, and one draw needn't show every extreme that they name: `contact`: tiles outside one band of consecutive slices, wrapping around the circumference, are 0. Over the tiles of one device (8 slices by 4 tiles), the pairs (owner, slot) are all distinct, so each device hands exactly 2 tiles to each index of gx. `slot`: see owner. `element_matrix`: symmetric.
All inputs are finite; a program needn't handle non-finite values.
Results may differ from the reference program's by a relative error of at most 0.00025.
Values sent between devices are 32-bit elements; how exact they have to be, the bound alone decides.
A program may use at most 128 MiB of HBM per device.

```python
import math
import jax
import jax.numpy as jnp
from jax import lax

CX = 8
CY = 256
CZ = 32
TW = 64
SWEEPS = 2
NX = 128
NY = 2048
NT = 32
CAP = 2


def draw_element_matrix(key, part):
    first_key = jax.random.fold_in(key, 1)
    second_key = jax.random.fold_in(key, 2)
    diagonal = jax.random.uniform(first_key, (24,), jnp.float32, 0.8, 1.2)
    spread = 0.06
    raw_values = jax.random.uniform(second_key, (24, 24), jnp.float32, -spread, spread)
    symmetric = 0.5 * (raw_values + raw_values.T)
    identity = jnp.arange(24)[:, None] == jnp.arange(24)[None, :]
    return jnp.where(identity, diagonal[:, None] * jnp.ones((24, 24), jnp.float32), symmetric)


def draw_precond(key, part):
    entries = []
    for index in range(9):
        entry_key = jax.random.fold_in(key, 10 + index)
        if index in (0, 4, 8):
            entries.append(jax.random.uniform(entry_key, (NX, CZ, NY), jnp.float32, 0.06, 0.14))
        else:
            entries.append(jax.random.uniform(entry_key, (NX, CZ, NY), jnp.float32, -0.03, 0.03))
    return jnp.stack(entries)


def draw_influence(key, part):
    shape = (NX // CX, NY // CY, NX // CX, CAP, TW, TW)
    diag_key = jax.random.fold_in(key, 31)
    off_key = jax.random.fold_in(key, 32)
    diagonal = jax.random.uniform(diag_key, shape[:5] + (1,), jnp.float32, 0.3, 0.6)
    others = jax.random.uniform(off_key, shape, jnp.float32, -1.0, 1.0) * (0.5 / TW)
    identity = jnp.arange(TW)[:, None] == jnp.arange(TW)[None, :]
    return jnp.where(identity, diagonal * jnp.ones(shape, jnp.float32), others)


def tile_codes(key):
    gx_count = NX // CX
    gy_count = NY // CY
    per_row = CY // TW
    tiles_dev = CX * per_row
    keys = jax.random.split(jax.random.fold_in(key, 7), gx_count * gy_count)
    perms = jax.vmap(lambda single: jax.random.permutation(single, tiles_dev))(keys)
    perms = perms.reshape(gx_count, gy_count, CX, per_row).transpose(0, 2, 1, 3).reshape(NX, NY // TW)
    return perms.astype(jnp.int32)


def draw_owner(key, part):
    return (tile_codes(key) // CAP).astype(jnp.int32)


def draw_slot(key, part):
    return (tile_codes(key) % CAP).astype(jnp.int32)


def draw_contact(key, part):
    center = jax.random.randint(jax.random.fold_in(key, 3), (), 0, NX)
    slices = jnp.arange(NX)
    distance = jnp.abs(slices - center)
    distance = jnp.minimum(distance, NX - distance)
    inside = distance < NX // 4
    picked = jax.random.randint(jax.random.fold_in(key, 5), (NX, NY // TW), 0, 8) < 7
    return (inside[:, None] & picked).astype(jnp.int32)


def steps_of(stream_key, dims, pieces, low, high):
    def one(dim, blocks):
        heights = jax.random.uniform(jax.random.fold_in(jax.random.fold_in(stream_key, 6), dim), (blocks,), jnp.float32, low / len(pieces), high / len(pieces))
        return jnp.repeat(jnp.exp(heights), dims[dim] // blocks).reshape((-1,) + (1,) * (len(dims) - dim - 1))

    loudness = one(*pieces[0])
    for cut in pieces[1:]:
        loudness = loudness * one(*cut)
    return loudness


def normal_values(rng, dims, width, limit, cuts=(), kind=jnp.bfloat16):
    array = width * jax.random.normal(rng, dims, jnp.float32)
    if cuts:
        array = array * steps_of(rng, dims, cuts, -0.22, 0.18)
    return jnp.clip(array, -limit, limit).astype(kind)


def setup_inputs(seed: int = 0) -> dict:
    splits = jax.random.split(jax.random.key(seed), 11)
    disp_start = normal_values(splits[0], (3, NX, CZ, NY), 1.0, 6.0, ((1, 16), (3, 8)), jnp.float32)
    load = normal_values(splits[1], (3, NX, CZ, NY), 4.0, 24.0, ((1, 16), (3, 8)), jnp.float32)
    modulus = jnp.clip(jnp.exp(math.log(2.0) - 1.3862944 * jax.random.uniform(splits[2], (NX, CZ, NY), jnp.float32) ** steps_of(splits[2], (NX, CZ, NY), ((0, 16), (2, 8)), -0.2, 0.2)), 0.5, 2.0)
    element_matrix = draw_element_matrix(jax.random.fold_in(splits[10], 71), 0)
    precond = draw_precond(jax.random.fold_in(splits[10], 71), 0)
    approach = jnp.clip(0.5 + 2.0 * jax.random.uniform(splits[5], (NX,), jnp.float32) ** steps_of(splits[5], (NX,), ((0, 16),), -0.2, 0.2), 0.5, 2.5)
    contact = draw_contact(jax.random.fold_in(splits[10], 71), 0)
    owner = draw_owner(jax.random.fold_in(splits[10], 71), 0)
    slot = draw_slot(jax.random.fold_in(splits[10], 71), 0)
    influence = draw_influence(jax.random.fold_in(splits[10], 71), 0)
    return dict(disp_start=disp_start, load=load, modulus=modulus, element_matrix=element_matrix, precond=precond, approach=approach, contact=contact, owner=owner, slot=slot, influence=influence)


penalty = 1.5
crown_depth = 0.4
crown_shape = 0.96


def element_apply(field_pad, coef_pad, stiffness):
    size_x, size_z, size_y = coef_pad.shape
    elem_x, elem_z, elem_y = size_x - 1, size_z - 1, size_y - 1
    columns = []
    for offset_x in (0, 1):
        for offset_y in (0, 1):
            for offset_z in (0, 1):
                for component in range(3):
                    columns.append(field_pad[component, offset_x:offset_x + elem_x, offset_z:offset_z + elem_z, offset_y:offset_y + elem_y])
    stacked = jnp.stack(columns)
    factor = coef_pad[:elem_x, :elem_z, :elem_y]
    total = jnp.zeros((3, size_x - 2, size_z, size_y - 2), jnp.float32)
    for offset_x in (0, 1):
        for offset_y in (0, 1):
            for offset_z in (0, 1):
                corner = 4 * offset_x + 2 * offset_y + offset_z
                rows = stiffness[3 * corner:3 * corner + 3]
                piece = jnp.einsum('ab,bxzy->axzy', rows, stacked, precision=lax.Precision.HIGHEST) * factor
                piece = jnp.pad(piece, ((0, 0), (0, 0), (1, 1), (0, 0)))
                total = total + piece[:, 1 - offset_x:size_x - 1 - offset_x, 1 - offset_z:1 - offset_z + size_z, 1 - offset_y:size_y - 1 - offset_y]
    return total


def block_apply(precond, resid):
    return jnp.stack([precond[3 * row] * resid[0] + precond[3 * row + 1] * resid[1] + precond[3 * row + 2] * resid[2] for row in range(3)])


def reference(disp_start, load, modulus, element_matrix, precond, approach, contact, owner, slot, influence):
    valid_x = (jnp.arange(NX) < NX - 1)[:, None, None]
    valid_z = (jnp.arange(CZ) < CZ - 1)[None, :, None]
    valid_y = (jnp.arange(NY) < NY - 1)[None, None, :]
    coef = jnp.where(valid_x & valid_y & valid_z, modulus, jnp.float32(0.0))
    coef_pad = jnp.pad(coef, ((1, 1), (0, 0), (1, 1)))
    starts = (jnp.arange(NX // CX) * CX).astype(jnp.int32)
    zero = jnp.zeros((), jnp.int32)

    def operate(field):
        field_pad = jnp.pad(field, ((0, 0), (1, 1), (0, 0), (1, 1)))

        def one_block(start):
            part_field = lax.dynamic_slice(field_pad, (zero, start, zero, zero), (3, CX + 2, CZ, NY + 2))
            part_coef = lax.dynamic_slice(coef_pad, (start, zero, zero), (CX + 2, CZ, NY + 2))
            return element_apply(part_field, part_coef, element_matrix)

        blocks = lax.map(one_block, starts)
        return jnp.transpose(blocks, (1, 0, 2, 3, 4)).reshape(3, NX, CZ, NY)

    relaxed = disp_start
    for sweep in range(SWEEPS):
        relaxed = relaxed + block_apply(precond, load - operate(relaxed))

    spread = (jnp.arange(NY).astype(jnp.float32) + 0.5) / NY * 2.0 - 1.0
    crown = -crown_depth * jnp.log(1.0 - crown_shape * spread * spread)
    penetration = approach[:, None] - crown[None, :] - relaxed[2, :, CZ - 1, :]
    tiles = penetration.reshape(NX, NT, TW)
    home_block = (jnp.arange(NX) // CX).astype(jnp.int32)[:, None]
    axial_block = (jnp.arange(NT) // (CY // TW)).astype(jnp.int32)[None, :]
    matrices = influence[owner, axial_block, home_block, slot]
    trial = penalty * jnp.maximum(tiles, 0.0)
    corrected = tiles - jnp.einsum('xtij,xtj->xti', matrices, trial, precision=lax.Precision.HIGHEST)
    pressure_tiles = penalty * jnp.maximum(corrected, 0.0) * contact[:, :, None].astype(jnp.float32)
    pressure = pressure_tiles.reshape(NX, NY)
    surface_gain = jnp.stack([precond[3 * row + 2, :, CZ - 1, :] for row in range(3)])
    displacement = relaxed.at[:, :, CZ - 1, :].add(-surface_gain * pressure[None])
    return displacement, pressure
```

```python
import functools

import jax
import jax.numpy as jnp
import numpy as np
from jax import lax
from jax.experimental import pallas as pl
from jax.experimental.pallas import tpu as pltpu
from jax.sharding import PartitionSpec as P

MESH = pl.DeviceIdType.MESH
F32 = jnp.float32
BF16 = jnp.bfloat16

TW = 64
PITCH = 10
penalty = 1.5
crown_depth = 0.4
crown_shape = 0.96

ROWS, HALF, COLS = 384, 192, 112


def tables():
    row = np.arange(ROWS)
    layer, c_out, i_out = row % 16, row // 16 % 2, row // 32 % 3
    b_out, a_out = row // 96 % 2, row // 192
    source = 3 * (4 * a_out + 2 * b_out + c_out) + i_out
    col = np.arange(2 * COLS)
    a_in, inner = col // COLS, col % COLS
    main = inner < 96
    node = np.where(main, inner % 16, np.where(inner < 102, 16, np.where(inner < 108, -1, -100)))
    which = np.where(main, inner // 16, (inner - 96) % 6)
    b_in, i_in = which // 3, which % 3
    dof = np.arange(24)
    pick_rows = source[:, None] == dof[None, :]
    pick_cols = np.concatenate(
        [dof[:, None] == (3 * (4 * a_in + 2 * b_in + c) + i_in)[None, :] for c in (0, 1)], axis=1
    )
    band = np.concatenate(
        [node[None, :] - layer[:, None] + c_out[:, None] == c for c in (0, 1)], axis=1
    )
    return tuple(jnp.asarray(t.astype(np.float32), BF16) for t in (pick_rows, pick_cols, band))


def split(value):
    high = value.astype(BF16)
    return high, (value - high.astype(F32)).astype(BF16)


def mm(a, b):
    return jnp.dot(a, b, preferred_element_type=F32)


def kernel(
    ngx, ngy,
    disp, load, modulus, emat, precond, approach, contact, owner, slot, influence,
    pick_rows, pick_cols, band,
    out_hbm, press_hbm,
    u1, u2, res1, res2, pre, mod, coef0, coef1, s_hi, s_lo, g_hi, g_lo,
    ext_hi, ext_lo, ext0, ext1, tot, out, press,
    em_v, rows_v, cols_v, band_v, app_v, con_v, own_v, slot_v, infl, w_hi, w_lo,
    msg_r1, msg_l1, msg_r2, msg_l2, in_r1, in_l1, in_r2, in_l2,
    send_a, recv_a, send_b, recv_b,
    local_sem, halo_send, halo_recv, a_send, a_recv, b_send, b_recv,
):
    gx, gy = lax.axis_index("gx"), lax.axis_index("gy")
    up_x, down_x = lax.rem(gx + 1, ngx), lax.rem(gx + ngx - 1, ngx)
    up_y, down_y = lax.rem(gy + 1, ngy), lax.rem(gy + ngy - 1, ngy)

    def local(i, src, dst):
        return pltpu.make_async_copy(src, dst, local_sem.at[i])

    loads = [
        local(0, disp, u1.at[:, pl.ds(1, 8)]),
        local(1, modulus, mod.at[pl.ds(1, 8)]),
        local(2, emat, em_v),
        local(3, pick_rows, rows_v),
        local(4, pick_cols, cols_v),
        local(5, band, band_v),
        local(6, load, res1),
        local(7, precond, pre),
        local(8, load, res2),
        local(9, approach, app_v),
        local(10, contact, con_v),
        local(11, owner, own_v),
        local(12, slot, slot_v),
        local(13, influence, infl),
    ]
    for c in loads:
        c.start()

    barrier = pltpu.get_barrier_semaphore()

    def greet(d, carry):
        pl.semaphore_signal(barrier, inc=1, device_id=(lax.rem(gx + d, ngx), gy), device_id_type=MESH)
        return carry

    lax.fori_loop(1, ngx, greet, 0)
    for oy in (up_y, down_y):
        for ox in (down_x, gx, up_x):
            pl.semaphore_signal(barrier, inc=1, device_id=(ox, oy), device_id_type=MESH)

    lane8 = lax.broadcasted_iota(jnp.int32, (8, 128), 1)
    lane16 = lax.broadcasted_iota(jnp.int32, (16, 128), 1)
    row16 = lax.broadcasted_iota(jnp.int32, (16, 256), 0)

    for i in (2, 3, 4, 5):
        loads[i].wait()
    for part, dst in zip(split(em_v[...]), (g_hi, g_lo)):
        wide = mm(mm(rows_v[...], part).astype(BF16), cols_v[...])
        dst[...] = (
            wide[:, : 2 * COLS] * band_v[:, : 2 * COLS].astype(F32)
            + wide[:, 2 * COLS :] * band_v[:, 2 * COLS :].astype(F32)
        ).astype(BF16)

    def pack(n, u, carry):
        left, right = carry
        for i in range(3):
            for k in range(4):
                base = (i * 4 + k) * PITCH
                hit = lane8 == base + n
                first = u[i, n, 8 * k : 8 * k + 8, 0:128]
                last = u[i, n, 8 * k : 8 * k + 8, 128:256]
                left = jnp.where(hit, pltpu.roll(first, base + n, axis=1), left)
                right = jnp.where(hit, pltpu.roll(last, base + n + 1, axis=1), right)
        return left, right

    def pack_coef(n, carry):
        for k in range(4):
            base = k * PITCH
            last = mod[n, 8 * k : 8 * k + 8, 128:256]
            carry = jnp.where(lane8 == base + n, pltpu.roll(last, base + n + 1, axis=1), carry)
        return carry

    zero8 = jnp.zeros((8, 128), F32)
    loads[0].wait()
    left, right = lax.fori_loop(1, 9, lambda n, c: pack(n, u1, c), (zero8, zero8))
    loads[1].wait()
    own_coef = lax.fori_loop(1, 9, pack_coef, zero8)
    msg_l1[0] = left
    msg_r1[0] = right
    msg_r1[1] = own_coef

    def remote(i, src, dst, to):
        return pltpu.make_async_remote_copy(
            src_ref=src, dst_ref=dst, send_sem=halo_send.at[i], recv_sem=halo_recv.at[i],
            device_id=to, device_id_type=MESH,
        )

    def columns(first, msg_l, msg_r, in_l, in_r):
        copies = []
        for d, ox in ((0, up_x), (1, gx), (2, down_x)):
            copies.append(remote(first + d, msg_r, in_r.at[d], (ox, up_y)))
            copies.append(remote(first + 3 + d, msg_l, in_l.at[d], (ox, down_y)))
        return copies

    pl.semaphore_wait(barrier, ngx - 1 + 6)
    slices1 = [
        remote(0, disp.at[:, pl.ds(7, 1)], u1.at[:, pl.ds(0, 1)], (up_x, gy)),
        remote(1, disp.at[:, pl.ds(0, 1)], u1.at[:, pl.ds(9, 1)], (down_x, gy)),
        remote(2, modulus.at[pl.ds(7, 1)], mod.at[pl.ds(0, 1)], (up_x, gy)),
    ]
    cols1 = columns(3, msg_l1, msg_r1, in_l1, in_r1)
    for c in slices1 + cols1:
        c.start()

    inside = (lax.broadcasted_iota(jnp.int32, (32, 256), 0) < 31) & (
        lax.broadcasted_iota(jnp.int32, (32, 256), 1) < 255
    )
    low_x = jnp.where(gx > 0, 1.0, 0.0).astype(F32)
    high_x = jnp.where(gx < ngx - 1, 1.0, 0.0).astype(F32)
    low_y = jnp.where(gy > 0, 1.0, 0.0).astype(F32)
    high_y = jnp.where(gy < ngy - 1, 1.0, 0.0).astype(F32)

    def set_coef(e, gain):
        value = jnp.where(inside, mod[e] * gain, 0.0)
        coef0[e] = value
        coef1[e] = pltpu.roll(value, 1, axis=0)

    def some_coef(e, carry):
        set_coef(e, jnp.where(e == 8, high_x, 1.0))
        return carry

    lax.fori_loop(1, 9, some_coef, 0)

    def operand(n, u):
        edge = [jnp.zeros((16, 256), F32), jnp.zeros((16, 256), F32)]
        for i in range(3):
            here = u[i, n]
            for b in range(2):
                value = here if b == 0 else pltpu.roll(here, 255, axis=1)
                j = b * 3 + i
                high, low = split(value)
                for g in range(2):
                    s_hi[g, n, 16 * j : 16 * j + 16] = high[16 * g : 16 * g + 16]
                    s_lo[g, n, 16 * j : 16 * j + 16] = low[16 * g : 16 * g + 16]
                edge[0] = jnp.where(row16 == j, value[16:17], edge[0])
                edge[1] = jnp.where(row16 == 6 + j, value[15:16], edge[1])
        for g in range(2):
            high, low = split(edge[g])
            s_hi[g, n, 96:112] = high
            s_lo[g, n, 96:112] = low

    def all_operands(u):
        def one(n, carry):
            operand(n, u)
            return carry

        lax.fori_loop(1, 9, one, 0)

    def product(sh, sl, start, size):
        gh, gl = g_hi[start : start + size], g_lo[start : start + size]
        return mm(gh, sh) + mm(gl, sh) + mm(gh, sl)

    def elements(e, g, sides, res):
        zs = slice(16 * g, 16 * g + 16)
        sh = s_hi[g, pl.ds(e, 2)].reshape(2 * COLS, 256)
        sl = s_lo[g, pl.ds(e, 2)].reshape(2 * COLS, 256)
        c0, c1 = coef0[e, zs], coef1[e, zs]
        r = product(sh, sl, HALF * sides[0], HALF * len(sides))
        for k, a in enumerate(sides):
            for i in range(3):
                parts = []
                for b in range(2):
                    at = ((k * 2 + b) * 3 + i) * 32
                    parts.append(r[at : at + 16] * c0 + r[at + 16 : at + 32] * c1)
                x = e - 1 + a
                res[i, x, zs] = res[i, x, zs] - (parts[0] + pltpu.roll(parts[1], 1, axis=1))

    def interior(g, res):
        def one(e, carry):
            elements(e, g, (0, 1), res)
            return carry

        lax.fori_loop(1, 8, one, 0)

    starts = [k * PITCH for k in range(12)]
    at_low = functools.reduce(jnp.logical_or, [lane8 == s for s in starts])
    at_high = functools.reduce(jnp.logical_or, [lane8 == s + 9 for s in starts])

    def merged(below, here, above):
        value = jnp.where(at_low, pltpu.roll(below, 120, axis=1), here)
        return jnp.where(at_high, pltpu.roll(above, 8, axis=1), value)

    def both(left, right, k):
        return jnp.where(
            lane8 < 64,
            pltpu.roll(left, (128 - k * PITCH) % 128, axis=1),
            pltpu.roll(right, (192 - k * PITCH) % 128, axis=1),
        )

    def ends(left, right, in_l, in_r):
        beyond_low = merged(in_r[0, 0], in_r[1, 0], in_r[2, 0])
        beyond_high = merged(in_l[0, 0], in_l[1, 0], in_l[2, 0])
        rowm = lax.broadcasted_iota(jnp.int32, (16, 128), 0)
        for b, (lo, hi) in enumerate(((beyond_low, right), (left, beyond_high))):
            for i in range(3):
                j = b * 3 + i
                here = jnp.concatenate([both(lo, hi, i * 4 + k) for k in range(4)], axis=0)
                for a in range(2):
                    value = here if a == 0 else pltpu.roll(here, 127, axis=1)
                    high, low = split(value)
                    for g in range(2):
                        at = a * COLS + 16 * j
                        ext_hi[g, at : at + 16] = high[16 * g : 16 * g + 16]
                        ext_lo[g, at : at + 16] = low[16 * g : 16 * g + 16]
                    for g, (row, source) in enumerate(((j, 16), (6 + j, 15))):
                        tot[g, a] = jnp.where(rowm == row, value[source : source + 1], 0.0 if j == 0 else tot[g, a])
        for a in range(2):
            for g in range(2):
                high, low = split(tot[g, a])
                at = a * COLS + 96
                ext_hi[g, at : at + 16] = high
                ext_lo[g, at : at + 16] = low

    def end_coef(own_coef):
        beyond = merged(in_r1[0, 1], in_r1[1, 1], in_r1[2, 1])
        gain = jnp.where(lane8 < 9, low_y, jnp.where((lane8 >= 64) & (lane8 < 73), high_y, 0.0))
        gain = jnp.where((lane8 == 0) | (lane8 == 64), gain * low_x, gain)
        gain = jnp.where((lane8 == 8) | (lane8 == 72), gain * high_x, gain)
        value = jnp.concatenate([both(beyond, own_coef, k) * gain for k in range(4)], axis=0)
        value = jnp.where(lax.broadcasted_iota(jnp.int32, (32, 128), 0) < 31, value, 0.0)
        ext0[...] = value
        ext1[...] = pltpu.roll(value, 1, axis=0)

    def end_elements(g):
        zs = slice(16 * g, 16 * g + 16)
        r = product(ext_hi[g], ext_lo[g], 0, ROWS)
        c0, c1 = ext0[zs], ext1[zs]
        for i in range(3):
            parts = []
            for a in range(2):
                at_b0, at_b1 = (a * 6 + i) * 32, (a * 6 + 3 + i) * 32
                picked = jnp.where(lane16 < 64, r[at_b1 : at_b1 + 16], r[at_b0 : at_b0 + 16])
                shifted = jnp.where(lane16 < 64, r[at_b1 + 16 : at_b1 + 32], r[at_b0 + 16 : at_b0 + 32])
                parts.append(picked * c0 + shifted * c1)
            tot[g, i] = parts[0] + pltpu.roll(parts[1], 1, axis=1)

    def update(g, x, res, u, store):
        zs = slice(16 * g, 16 * g + 16)
        resid = []
        for i in range(3):
            sides = tot[g, i]
            low = jnp.where(lane16 == 0, pltpu.roll(sides, 127 - x, axis=1), 0.0)
            high = jnp.where(lane16 == 127, pltpu.roll(sides, 62 - x, axis=1), 0.0)
            resid.append(res[i, x, zs] - jnp.concatenate([low, high], axis=1))
        for i in range(3):
            value = u[i, x + 1, zs]
            for j in range(3):
                value = value + pre[3 * i + j, x, zs] * resid[j]
            store(i, x, zs, value)

    def update_all(g, res, u, store):
        def one(x, carry):
            update(g, x, res, u, store)
            return carry

        lax.fori_loop(0, 8, one, 0)

    all_operands(u1)
    loads[6].wait()
    for g in (1, 0):
        interior(g, res1)
    for c in slices1:
        c.wait_recv()
    set_coef(0, low_x)
    operand(0, u1)
    operand(9, u1)
    for g in (1, 0):
        elements(0, g, (1,), res1)
        elements(8, g, (0,), res1)
    left, right = pack(9, u1, pack(0, u1, (msg_l1[0], msg_r1[0])))
    own_coef = pack_coef(0, msg_r1[1])
    for c in cols1:
        c.wait_recv()
    ends(left, right, in_l1, in_r1)
    end_coef(own_coef)
    for g in (1, 0):
        end_elements(g)

    def store_u2(i, x, zs, value):
        u2[i, x + 1, zs] = value

    loads[7].wait()
    for g in (1, 0):
        update_all(g, res1, u1, store_u2)
    slices2 = [
        remote(9, u2.at[:, pl.ds(8, 1)], u2.at[:, pl.ds(0, 1)], (up_x, gy)),
        remote(10, u2.at[:, pl.ds(1, 1)], u2.at[:, pl.ds(9, 1)], (down_x, gy)),
    ]
    for c in slices2:
        c.start()
    left, right = lax.fori_loop(1, 9, lambda n, c: pack(n, u2, c), (zero8, zero8))
    msg_l2[0] = left
    msg_r2[0] = right
    cols2 = columns(11, msg_l2, msg_r2, in_l2, in_r2)
    for c in cols2:
        c.start()

    all_operands(u2)
    loads[8].wait()
    interior(1, res2)
    for c in slices2:
        c.wait_recv()
    operand(0, u2)
    operand(9, u2)
    left, right = pack(9, u2, pack(0, u2, (msg_l2[0], msg_r2[0])))
    for c in cols2:
        c.wait_recv()
    ends(left, right, in_l2, in_r2)
    elements(0, 1, (1,), res2)
    elements(8, 1, (0,), res2)
    end_elements(1)

    def store_out(i, x, zs, value):
        out[i, x, zs] = value

    update_all(1, res2, u2, store_out)

    for i in (9, 10, 11, 12):
        loads[i].wait()
    lane_a = lax.broadcasted_iota(jnp.int32, (8, 8), 1)
    diag = lane_a == lax.broadcasted_iota(jnp.int32, (8, 8), 0)
    gaps = jnp.sum(jnp.where(diag, jnp.broadcast_to(app_v[...], (8, 8)), 0.0), axis=1, keepdims=True)
    y_at = (gy * 256 + lax.broadcasted_iota(jnp.int32, (1, 256), 1)).astype(F32)
    spread = (y_at + 0.5) / (256.0 * ngy) * 2.0 - 1.0
    crown = -crown_depth * jnp.log(1.0 - crown_shape * spread * spread)
    surface = jnp.concatenate([out[2, x, 31:32] for x in range(8)], axis=0)
    pen = gaps - crown - surface

    def by_tile(ref):
        return jnp.concatenate([ref[:, t : t + 1] for t in range(4)], axis=0)

    owners, slots = by_tile(own_v), by_tile(slot_v)
    lane32 = lax.broadcasted_iota(jnp.int32, (32, 128), 1)
    is_first = slots == 0

    def rolled(v):
        return pltpu.roll(v, 64, axis=1)

    halves = [pen[:, :128], pen[:, 128:]]
    tiles = jnp.concatenate([halves[0], rolled(halves[0]), halves[1], rolled(halves[1])], axis=0)
    tiles = jnp.where(lane32 < 64, tiles, 0.0)
    tiles = jnp.where(is_first, tiles, rolled(tiles))

    def exact(one_hot, value, dims):
        high, rest = split(value)
        mid, low = split(value - high.astype(F32))
        total = None
        for part in (low, mid, high):
            term = lax.dot_general(one_hot, part, (dims, ((), ())), preferred_element_type=F32)
            total = term if total is None else total + term
        return total

    to_row = jnp.where(lane32 == owners * 8, 1.0, 0.0).astype(BF16)
    send_a[...] = exact(to_row, tiles, ((0,), (0,)))

    def ring(src, dst, ssem, rsem):
        def copy(d):
            peer = lax.rem(gx + d, ngx)
            return pltpu.make_async_remote_copy(
                src_ref=src.at[pl.ds(pl.multiple_of(peer * 8, 8), 8)],
                dst_ref=dst.at[pl.ds(pl.multiple_of(gx * 8, 8), 8)],
                send_sem=ssem.at[d], recv_sem=rsem.at[d],
                device_id=(peer, gy), device_id_type=MESH,
            )

        def own():
            at = pl.ds(pl.multiple_of(gx * 8, 8), 8)
            return pltpu.make_async_copy(src.at[at], dst.at[at], ssem.at[0])

        def start(d, carry):
            copy(d).start()
            return carry

        def wait_recv(d, carry):
            copy(d).wait_recv()
            return carry

        def wait_send(d, carry):
            copy(d).wait_send()
            return carry

        def start_all():
            lax.fori_loop(1, ngx, start, 0)
            own().start()

        def arrived():
            own().wait()
            lax.fori_loop(1, ngx, wait_recv, 0)

        return start_all, arrived, lambda: lax.fori_loop(1, ngx, wait_send, 0)

    go_a, arrived_a, sent_a = ring(send_a, recv_a, a_send, a_recv)
    go_b, arrived_b, sent_b = ring(send_b, recv_b, b_send, b_recv)
    go_a()

    interior(0, res2)
    elements(0, 0, (1,), res2)
    elements(8, 0, (0,), res2)
    end_elements(0)
    update_all(0, res2, u2, store_out)
    early = local(14, out.at[:, :, pl.ds(0, 24)], out_hbm.at[:, :, pl.ds(0, 24)])
    early.start()

    loads[13].wait()

    def prepare(k, carry):
        empty = jnp.zeros((TW, TW), F32)
        rows = jnp.concatenate(
            [
                jnp.concatenate([infl[2 * k], empty], axis=1),
                jnp.concatenate([empty, infl[2 * k + 1]], axis=1),
            ],
            axis=0,
        )
        w_hi[k], w_lo[k] = split(rows)
        return carry

    lax.fori_loop(0, ngx, prepare, 0)

    arrived_a()
    got = jnp.concatenate([recv_a[8 * k : 8 * k + 1] for k in range(16)], axis=0)
    trial = penalty * jnp.maximum(got, 0.0)
    t_hi, t_lo = split(trial)
    rowk = lax.broadcasted_iota(jnp.int32, (16, 128), 0)

    def nt(a, b):
        return lax.dot_general(a, b, (((1,), (1,)), ((), ())), preferred_element_type=F32)

    change = jnp.zeros((16, 128), F32)
    for k in range(16):
        term = nt(t_hi, w_hi[k]) + nt(t_lo, w_hi[k]) + nt(t_hi, w_lo[k])
        change = jnp.where(rowk == k, term, change)
    solved = penalty * jnp.maximum(got - change, 0.0)
    for k in range(16):
        send_b[8 * k : 8 * k + 8] = jnp.broadcast_to(solved[k : k + 1], (8, 128))
    go_b()

    gain_rows = [
        jnp.concatenate([pre[3 * i + 2, x, 31:32] for x in range(8)], axis=0) for i in range(3)
    ]
    top = [jnp.concatenate([out[i, x, 31:32] for x in range(8)], axis=0) for i in range(3)]
    on = by_tile(con_v).astype(F32)
    from_row = jnp.where(lax.broadcasted_iota(jnp.int32, (32, 16), 1) == owners, 1.0, 0.0).astype(BF16)
    arrived_b()
    back = jnp.concatenate([recv_b[8 * k : 8 * k + 1] for k in range(16)], axis=0)
    home = exact(from_row, back, ((1,), (0,)))
    home = jnp.where(is_first, home, rolled(home)) * on
    first = lane8 < 64
    value = jnp.concatenate(
        [
            jnp.where(first, home[0:8], rolled(home[8:16])),
            jnp.where(first, home[16:24], rolled(home[24:32])),
        ],
        axis=1,
    )
    press[...] = value
    for i in range(3):
        fixed = top[i] - gain_rows[i] * value
        for x in range(8):
            out[i, x, 31:32] = fixed[x : x + 1]
    late = [
        local(15, out.at[:, :, pl.ds(24, 8)], out_hbm.at[:, :, pl.ds(24, 8)]),
        local(16, press, press_hbm),
    ]
    for c in late:
        c.start()
    for c in slices1 + cols1 + slices2 + cols2:
        c.wait_send()
    sent_a()
    sent_b()
    early.wait()
    for c in late:
        c.wait()


def solution(mesh):
    ngx, ngy = mesh.shape["gx"], mesh.shape["gy"]

    def per_device(
        disp_start, load, modulus, element_matrix, precond, approach, contact, owner, slot, influence
    ):
        vm = lambda shape, dtype=F32: pltpu.VMEM(shape, dtype)
        dma = lambda n: pltpu.SemaphoreType.DMA((n,))
        anywhere = pl.BlockSpec(memory_space=pl.ANY)
        return pl.pallas_call(
            functools.partial(kernel, ngx, ngy),
            out_shape=(
                jax.ShapeDtypeStruct((3, 8, 32, 256), F32),
                jax.ShapeDtypeStruct((8, 256), F32),
            ),
            in_specs=[anywhere] * 13,
            out_specs=(anywhere, anywhere),
            scratch_shapes=[
                vm((3, 10, 32, 256)), vm((3, 10, 32, 256)),
                vm((3, 8, 32, 256)), vm((3, 8, 32, 256)), vm((9, 8, 32, 256)),
                vm((9, 32, 256)), vm((9, 32, 256)), vm((9, 32, 256)),
                vm((2, 10, COLS, 256), BF16), vm((2, 10, COLS, 256), BF16),
                vm((ROWS, 2 * COLS), BF16), vm((ROWS, 2 * COLS), BF16),
                vm((2, 2 * COLS, 128), BF16), vm((2, 2 * COLS, 128), BF16),
                vm((32, 128)), vm((32, 128)), vm((2, 3, 16, 128)),
                vm((3, 8, 32, 256)), vm((8, 256)),
                vm((24, 24)), vm((ROWS, 24), BF16), vm((24, 4 * COLS), BF16), vm((ROWS, 4 * COLS), BF16),
                vm((1, 8)), vm((8, 4), jnp.int32), vm((8, 4), jnp.int32), vm((8, 4), jnp.int32),
                vm((32, TW, TW)), vm((16, 128, 128), BF16), vm((16, 128, 128), BF16),
                vm((2, 8, 128)), vm((1, 8, 128)), vm((1, 8, 128)), vm((1, 8, 128)),
                vm((3, 2, 8, 128)), vm((3, 1, 8, 128)), vm((3, 1, 8, 128)), vm((3, 1, 8, 128)),
                vm((128, 128)), vm((128, 128)), vm((128, 128)), vm((128, 128)),
                dma(17), dma(17), dma(17), dma(16), dma(16), dma(16), dma(16),
            ],
            compiler_params=pltpu.CompilerParams(
                collective_id=0, has_side_effects=True, vmem_limit_bytes=48 * 1024 * 1024
            ),
        )(
            disp_start, load, modulus, element_matrix, precond, approach.reshape(1, 8),
            contact, owner, slot, influence.reshape(32, TW, TW), *tables(),
        )

    return jax.shard_map(
        per_device,
        mesh=mesh,
        in_specs=(
            P(None, "gx", None, "gy"),
            P(None, "gx", None, "gy"),
            P("gx", None, "gy"),
            P(),
            P(None, "gx", None, "gy"),
            P("gx"),
            P("gx", "gy"),
            P("gx", "gy"),
            P("gx", "gy"),
            P("gx", "gy", None, None, None, None),
        ),
        out_specs=(P(None, "gx", None, "gy"), P("gx", "gy")),
        check_vma=False,
    )
```

```python
import functools

import jax
import jax.numpy as jnp
import numpy as np
from jax import lax
from jax.experimental import pallas as pl
from jax.experimental.pallas import tpu as pltpu
from jax.sharding import PartitionSpec as P

MESH = pl.DeviceIdType.MESH
F32 = jnp.float32
BF16 = jnp.bfloat16

TW = 64
PITCH = 10
penalty = 1.5
crown_depth = 0.4
crown_shape = 0.96

ROWS, HALF, COLS = 384, 192, 112


def tables():
    row = np.arange(ROWS)
    layer, c_out, i_out = row % 16, row // 16 % 2, row // 32 % 3
    b_out, a_out = row // 96 % 2, row // 192
    source = 3 * (4 * a_out + 2 * b_out + c_out) + i_out
    col = np.arange(2 * COLS)
    a_in, inner = col // COLS, col % COLS
    main = inner < 96
    node = np.where(main, inner % 16, np.where(inner < 102, 16, np.where(inner < 108, -1, -100)))
    which = np.where(main, inner // 16, (inner - 96) % 6)
    b_in, i_in = which // 3, which % 3
    dof = np.arange(24)
    pick_rows = source[:, None] == dof[None, :]
    pick_cols = np.concatenate(
        [dof[:, None] == (3 * (4 * a_in + 2 * b_in + c) + i_in)[None, :] for c in (0, 1)], axis=1
    )
    band = np.concatenate(
        [node[None, :] - layer[:, None] + c_out[:, None] == c for c in (0, 1)], axis=1
    )
    return tuple(jnp.asarray(t.astype(np.float32), BF16) for t in (pick_rows, pick_cols, band))


def split(value):
    high = value.astype(BF16)
    return high, (value - high.astype(F32)).astype(BF16)


def mm(a, b):
    return jnp.dot(a, b, preferred_element_type=F32)


def kernel(
    ngx, ngy,
    disp, load, modulus, emat, precond, approach, contact, owner, slot, influence,
    pick_rows, pick_cols, band,
    out_hbm, press_hbm,
    u1, u2, res1, res2, pre, mod, coef0, coef1, s_hi, s_lo, g_hi, g_lo,
    ext_hi, ext_lo, ext0, ext1, tot, out, press,
    em_v, rows_v, cols_v, band_v, app_v, con_v, own_v, slot_v, infl, w_hi, w_lo,
    msg_r1, msg_l1, msg_r2, msg_l2, in_r1, in_l1, in_r2, in_l2,
    send_a, recv_a, send_b, recv_b,
    local_sem, halo_send, halo_recv, a_send, a_recv, b_send, b_recv,
):
    gx, gy = lax.axis_index("gx"), lax.axis_index("gy")
    up_x, down_x = lax.rem(gx + 1, ngx), lax.rem(gx + ngx - 1, ngx)
    up_y, down_y = lax.rem(gy + 1, ngy), lax.rem(gy + ngy - 1, ngy)

    def local(i, src, dst):
        return pltpu.make_async_copy(src, dst, local_sem.at[i])

    loads = [
        local(0, disp, u1.at[:, pl.ds(1, 8)]),
        local(1, modulus, mod.at[pl.ds(1, 8)]),
        local(2, emat, em_v),
        local(3, pick_rows, rows_v),
        local(4, pick_cols, cols_v),
        local(5, band, band_v),
        local(6, load, res1),
        local(7, precond, pre),
        local(8, load, res2),
        local(9, approach, app_v),
        local(10, contact, con_v),
        local(11, owner, own_v),
        local(12, slot, slot_v),
        local(13, influence, infl),
    ]
    for c in loads[:2]:
        c.start()

    barrier = pltpu.get_barrier_semaphore()

    def greet(d, carry):
        pl.semaphore_signal(barrier, inc=1, device_id=(lax.rem(gx + d, ngx), gy), device_id_type=MESH)
        return carry

    lax.fori_loop(1, ngx, greet, 0, unroll=True)
    for oy in (up_y, down_y):
        for ox in (down_x, gx, up_x):
            pl.semaphore_signal(barrier, inc=1, device_id=(ox, oy), device_id_type=MESH)

    def remote(i, src, dst, to):
        return pltpu.make_async_remote_copy(
            src_ref=src, dst_ref=dst, send_sem=halo_send.at[i], recv_sem=halo_recv.at[i],
            device_id=to, device_id_type=MESH,
        )

    pl.semaphore_wait(barrier, ngx - 1 + 6)
    slices1 = [
        remote(0, disp.at[:, pl.ds(7, 1)], u1.at[:, pl.ds(0, 1)], (up_x, gy)),
        remote(1, disp.at[:, pl.ds(0, 1)], u1.at[:, pl.ds(9, 1)], (down_x, gy)),
        remote(2, modulus.at[pl.ds(7, 1)], mod.at[pl.ds(0, 1)], (up_x, gy)),
    ]
    for c in slices1:
        c.start()
    for c in loads[2:]:
        c.start()

    lane8 = lax.broadcasted_iota(jnp.int32, (8, 128), 1)
    lane16 = lax.broadcasted_iota(jnp.int32, (16, 128), 1)
    row16 = lax.broadcasted_iota(jnp.int32, (16, 256), 0)

    def pack(n, u, carry):
        left, right = carry
        for i in range(3):
            for k in range(4):
                base = (i * 4 + k) * PITCH
                hit = lane8 == base + n
                first = u[i, n, 8 * k : 8 * k + 8, 0:128]
                last = u[i, n, 8 * k : 8 * k + 8, 128:256]
                left = jnp.where(hit, pltpu.roll(first, base + n, axis=1), left)
                right = jnp.where(hit, pltpu.roll(last, base + n + 1, axis=1), right)
        return left, right

    def pack_coef(n, carry):
        for k in range(4):
            base = k * PITCH
            last = mod[n, 8 * k : 8 * k + 8, 128:256]
            carry = jnp.where(lane8 == base + n, pltpu.roll(last, base + n + 1, axis=1), carry)
        return carry

    zero8 = jnp.zeros((8, 128), F32)
    loads[0].wait()
    left, right = lax.fori_loop(1, 9, lambda n, c: pack(n, u1, c), (zero8, zero8), unroll=True)
    loads[1].wait()
    own_coef = lax.fori_loop(1, 9, pack_coef, zero8, unroll=True)
    msg_l1[0] = left
    msg_r1[0] = right
    msg_r1[1] = own_coef

    def columns(first, msg_l, msg_r, in_l, in_r):
        copies = []
        for d, ox in ((0, up_x), (1, gx), (2, down_x)):
            copies.append(remote(first + d, msg_r, in_r.at[d], (ox, up_y)))
            copies.append(remote(first + 3 + d, msg_l, in_l.at[d], (ox, down_y)))
        return copies

    cols1 = columns(3, msg_l1, msg_r1, in_l1, in_r1)
    for c in cols1:
        c.start()

    for i in (2, 3, 4, 5):
        loads[i].wait()
    for part, dst in zip(split(em_v[...]), (g_hi, g_lo)):
        wide = mm(mm(rows_v[...], part).astype(BF16), cols_v[...])
        dst[...] = (
            wide[:, : 2 * COLS] * band_v[:, : 2 * COLS].astype(F32)
            + wide[:, 2 * COLS :] * band_v[:, 2 * COLS :].astype(F32)
        ).astype(BF16)

    inside = (lax.broadcasted_iota(jnp.int32, (32, 256), 0) < 31) & (
        lax.broadcasted_iota(jnp.int32, (32, 256), 1) < 255
    )
    low_x = jnp.where(gx > 0, 1.0, 0.0).astype(F32)
    high_x = jnp.where(gx < ngx - 1, 1.0, 0.0).astype(F32)
    low_y = jnp.where(gy > 0, 1.0, 0.0).astype(F32)
    high_y = jnp.where(gy < ngy - 1, 1.0, 0.0).astype(F32)

    def set_coef(e, gain):
        value = jnp.where(inside, mod[e] * gain, 0.0)
        coef0[e] = value
        coef1[e] = pltpu.roll(value, 1, axis=0)

    def some_coef(e, carry):
        set_coef(e, jnp.where(e == 8, high_x, 1.0))
        return carry

    lax.fori_loop(1, 9, some_coef, 0, unroll=True)

    def operand(n, u):
        edge = [jnp.zeros((16, 256), F32), jnp.zeros((16, 256), F32)]
        for i in range(3):
            here = u[i, n]
            for b in range(2):
                value = here if b == 0 else pltpu.roll(here, 255, axis=1)
                j = b * 3 + i
                high, low = split(value)
                for g in range(2):
                    s_hi[g, n, 16 * j : 16 * j + 16] = high[16 * g : 16 * g + 16]
                    s_lo[g, n, 16 * j : 16 * j + 16] = low[16 * g : 16 * g + 16]
                edge[0] = jnp.where(row16 == j, value[16:17], edge[0])
                edge[1] = jnp.where(row16 == 6 + j, value[15:16], edge[1])
        for g in range(2):
            high, low = split(edge[g])
            s_hi[g, n, 96:112] = high
            s_lo[g, n, 96:112] = low

    def all_operands(u):
        def one(n, carry):
            operand(n, u)
            return carry

        lax.fori_loop(1, 9, one, 0, unroll=True)

    def product(sh, sl, start, size):
        gh, gl = g_hi[start : start + size], g_lo[start : start + size]
        return mm(gh, sh) + mm(gl, sh) + mm(gh, sl)

    def elements(e, g, sides, res):
        zs = slice(16 * g, 16 * g + 16)
        sh = s_hi[g, pl.ds(e, 2)].reshape(2 * COLS, 256)
        sl = s_lo[g, pl.ds(e, 2)].reshape(2 * COLS, 256)
        c0, c1 = coef0[e, zs], coef1[e, zs]
        r = product(sh, sl, HALF * sides[0], HALF * len(sides))
        for k, a in enumerate(sides):
            for i in range(3):
                parts = []
                for b in range(2):
                    at = ((k * 2 + b) * 3 + i) * 32
                    parts.append(r[at : at + 16] * c0 + r[at + 16 : at + 32] * c1)
                x = e - 1 + a
                res[i, x, zs] = res[i, x, zs] - (parts[0] + pltpu.roll(parts[1], 1, axis=1))

    def interior(g, res):
        def one(e, carry):
            elements(e, g, (0, 1), res)
            return carry

        lax.fori_loop(1, 8, one, 0, unroll=True)

    starts = [k * PITCH for k in range(12)]
    at_low = functools.reduce(jnp.logical_or, [lane8 == s for s in starts])
    at_high = functools.reduce(jnp.logical_or, [lane8 == s + 9 for s in starts])

    def merged(below, here, above):
        value = jnp.where(at_low, pltpu.roll(below, 120, axis=1), here)
        return jnp.where(at_high, pltpu.roll(above, 8, axis=1), value)

    def both(left, right, k):
        return jnp.where(
            lane8 < 64,
            pltpu.roll(left, (128 - k * PITCH) % 128, axis=1),
            pltpu.roll(right, (192 - k * PITCH) % 128, axis=1),
        )

    def ends(left, right, in_l, in_r):
        beyond_low = merged(in_r[0, 0], in_r[1, 0], in_r[2, 0])
        beyond_high = merged(in_l[0, 0], in_l[1, 0], in_l[2, 0])
        rowm = lax.broadcasted_iota(jnp.int32, (16, 128), 0)
        for b, (lo, hi) in enumerate(((beyond_low, right), (left, beyond_high))):
            for i in range(3):
                j = b * 3 + i
                here = jnp.concatenate([both(lo, hi, i * 4 + k) for k in range(4)], axis=0)
                for a in range(2):
                    value = here if a == 0 else pltpu.roll(here, 127, axis=1)
                    high, low = split(value)
                    for g in range(2):
                        at = a * COLS + 16 * j
                        ext_hi[g, at : at + 16] = high[16 * g : 16 * g + 16]
                        ext_lo[g, at : at + 16] = low[16 * g : 16 * g + 16]
                    for g, (row, source) in enumerate(((j, 16), (6 + j, 15))):
                        tot[g, a] = jnp.where(rowm == row, value[source : source + 1], 0.0 if j == 0 else tot[g, a])
        for a in range(2):
            for g in range(2):
                high, low = split(tot[g, a])
                at = a * COLS + 96
                ext_hi[g, at : at + 16] = high
                ext_lo[g, at : at + 16] = low

    def end_coef(own_coef):
        beyond = merged(in_r1[0, 1], in_r1[1, 1], in_r1[2, 1])
        gain = jnp.where(lane8 < 9, low_y, jnp.where((lane8 >= 64) & (lane8 < 73), high_y, 0.0))
        gain = jnp.where((lane8 == 0) | (lane8 == 64), gain * low_x, gain)
        gain = jnp.where((lane8 == 8) | (lane8 == 72), gain * high_x, gain)
        value = jnp.concatenate([both(beyond, own_coef, k) * gain for k in range(4)], axis=0)
        value = jnp.where(lax.broadcasted_iota(jnp.int32, (32, 128), 0) < 31, value, 0.0)
        ext0[...] = value
        ext1[...] = pltpu.roll(value, 1, axis=0)

    def end_elements(g):
        zs = slice(16 * g, 16 * g + 16)
        r = product(ext_hi[g], ext_lo[g], 0, ROWS)
        c0, c1 = ext0[zs], ext1[zs]
        for i in range(3):
            parts = []
            for a in range(2):
                at_b0, at_b1 = (a * 6 + i) * 32, (a * 6 + 3 + i) * 32
                picked = jnp.where(lane16 < 64, r[at_b1 : at_b1 + 16], r[at_b0 : at_b0 + 16])
                shifted = jnp.where(lane16 < 64, r[at_b1 + 16 : at_b1 + 32], r[at_b0 + 16 : at_b0 + 32])
                parts.append(picked * c0 + shifted * c1)
            tot[g, i] = parts[0] + pltpu.roll(parts[1], 1, axis=1)

    def update(g, x, res, u, store):
        zs = slice(16 * g, 16 * g + 16)
        resid = []
        for i in range(3):
            sides = tot[g, i]
            low = jnp.where(lane16 == 0, pltpu.roll(sides, 127 - x, axis=1), 0.0)
            high = jnp.where(lane16 == 127, pltpu.roll(sides, 62 - x, axis=1), 0.0)
            resid.append(res[i, x, zs] - jnp.concatenate([low, high], axis=1))
        for i in range(3):
            value = u[i, x + 1, zs]
            for j in range(3):
                value = value + pre[3 * i + j, x, zs] * resid[j]
            store(i, x, zs, value)

    def update_all(g, res, u, store):
        def one(x, carry):
            update(g, x, res, u, store)
            return carry

        lax.fori_loop(0, 8, one, 0, unroll=True)

    all_operands(u1)
    loads[6].wait()
    for g in (1, 0):
        interior(g, res1)
    for c in slices1:
        c.wait_recv()
    set_coef(0, low_x)
    operand(0, u1)
    operand(9, u1)
    for g in (1, 0):
        elements(0, g, (1,), res1)
        elements(8, g, (0,), res1)
    left, right = pack(9, u1, pack(0, u1, (msg_l1[0], msg_r1[0])))
    own_coef = pack_coef(0, msg_r1[1])
    for c in cols1:
        c.wait_recv()
    ends(left, right, in_l1, in_r1)
    end_coef(own_coef)
    for g in (1, 0):
        end_elements(g)

    def store_u2(i, x, zs, value):
        u2[i, x + 1, zs] = value

    loads[7].wait()
    for g in (1, 0):
        update_all(g, res1, u1, store_u2)
    slices2 = [
        remote(9, u2.at[:, pl.ds(8, 1)], u2.at[:, pl.ds(0, 1)], (up_x, gy)),
        remote(10, u2.at[:, pl.ds(1, 1)], u2.at[:, pl.ds(9, 1)], (down_x, gy)),
    ]
    for c in slices2:
        c.start()
    left, right = lax.fori_loop(1, 9, lambda n, c: pack(n, u2, c), (zero8, zero8), unroll=True)
    msg_l2[0] = left
    msg_r2[0] = right
    cols2 = columns(11, msg_l2, msg_r2, in_l2, in_r2)
    for c in cols2:
        c.start()

    all_operands(u2)
    loads[8].wait()
    interior(1, res2)
    for c in slices2:
        c.wait_recv()
    operand(0, u2)
    operand(9, u2)
    left, right = pack(9, u2, pack(0, u2, (msg_l2[0], msg_r2[0])))
    for c in cols2:
        c.wait_recv()
    ends(left, right, in_l2, in_r2)
    elements(0, 1, (1,), res2)
    elements(8, 1, (0,), res2)
    end_elements(1)

    def store_out(i, x, zs, value):
        out[i, x, zs] = value

    update_all(1, res2, u2, store_out)

    for i in (9, 10, 11, 12):
        loads[i].wait()
    lane_a = lax.broadcasted_iota(jnp.int32, (8, 8), 1)
    diag = lane_a == lax.broadcasted_iota(jnp.int32, (8, 8), 0)

    def upright(row):
        return jnp.sum(jnp.where(diag, jnp.broadcast_to(row, (8, 8)), 0.0), axis=1, keepdims=True)

    gaps = upright(app_v[...])
    y_at = (gy * 256 + lax.broadcasted_iota(jnp.int32, (1, 256), 1)).astype(F32)
    spread = (y_at + 0.5) / (256.0 * ngy) * 2.0 - 1.0
    crown = -crown_depth * jnp.log(1.0 - crown_shape * spread * spread)
    surface = jnp.concatenate([out[2, x, 31:32] for x in range(8)], axis=0)
    pen = gaps - crown - surface

    def by_tile(ref):
        value = ref[...].astype(F32)
        return jnp.concatenate([upright(value[t : t + 1]) for t in range(4)], axis=0)

    owners = by_tile(own_v).astype(jnp.int32)
    slots = by_tile(slot_v)
    lane32 = lax.broadcasted_iota(jnp.int32, (32, 128), 1)
    is_first = slots == 0

    def rolled(v):
        return pltpu.roll(v, 64, axis=1)

    halves = [pen[:, :128], pen[:, 128:]]
    tiles = jnp.concatenate([halves[0], rolled(halves[0]), halves[1], rolled(halves[1])], axis=0)
    tiles = jnp.where(lane32 < 64, tiles, 0.0)
    tiles = jnp.where(is_first, tiles, rolled(tiles))

    def exact(one_hot, value, dims):
        high, rest = split(value)
        mid, low = split(value - high.astype(F32))
        total = None
        for part in (low, mid, high):
            term = lax.dot_general(one_hot, part, (dims, ((), ())), preferred_element_type=F32)
            total = term if total is None else total + term
        return total

    to_row = jnp.where(lane32 == owners * 8, 1.0, 0.0).astype(BF16)
    send_a[...] = exact(to_row, tiles, ((0,), (0,)))

    def ring(src, dst, ssem, rsem):
        def copy(d):
            peer = lax.rem(gx + d, ngx)
            return pltpu.make_async_remote_copy(
                src_ref=src.at[pl.ds(pl.multiple_of(peer * 8, 8), 8)],
                dst_ref=dst.at[pl.ds(pl.multiple_of(gx * 8, 8), 8)],
                send_sem=ssem.at[d], recv_sem=rsem.at[d],
                device_id=(peer, gy), device_id_type=MESH,
            )

        def own():
            at = pl.ds(pl.multiple_of(gx * 8, 8), 8)
            return pltpu.make_async_copy(src.at[at], dst.at[at], ssem.at[0])

        def start(d, carry):
            copy(d).start()
            return carry

        def wait_recv(d, carry):
            copy(d).wait_recv()
            return carry

        def wait_send(d, carry):
            copy(d).wait_send()
            return carry

        def start_all():
            lax.fori_loop(1, ngx, start, 0, unroll=True)
            own().start()

        def arrived():
            own().wait()
            lax.fori_loop(1, ngx, wait_recv, 0, unroll=True)

        return start_all, arrived, lambda: lax.fori_loop(1, ngx, wait_send, 0, unroll=True)

    go_a, arrived_a, sent_a = ring(send_a, recv_a, a_send, a_recv)
    go_b, arrived_b, sent_b = ring(send_b, recv_b, b_send, b_recv)
    go_a()

    interior(0, res2)
    elements(0, 0, (1,), res2)
    elements(8, 0, (0,), res2)
    end_elements(0)
    update_all(0, res2, u2, store_out)
    early = local(14, out.at[:, :, pl.ds(0, 24)], out_hbm.at[:, :, pl.ds(0, 24)])
    early.start()

    loads[13].wait()

    def prepare(k, carry):
        empty = jnp.zeros((TW, TW), F32)
        rows = jnp.concatenate(
            [
                jnp.concatenate([infl[2 * k], empty], axis=1),
                jnp.concatenate([empty, infl[2 * k + 1]], axis=1),
            ],
            axis=0,
        )
        w_hi[k], w_lo[k] = split(rows)
        return carry

    lax.fori_loop(0, ngx, prepare, 0, unroll=True)

    arrived_a()
    got = jnp.concatenate([recv_a[8 * k : 8 * k + 1] for k in range(16)], axis=0)
    trial = penalty * jnp.maximum(got, 0.0)
    t_hi, t_lo = split(trial)
    rowk = lax.broadcasted_iota(jnp.int32, (16, 128), 0)

    def nt(a, b):
        return lax.dot_general(a, b, (((1,), (1,)), ((), ())), preferred_element_type=F32)

    change = jnp.zeros((16, 128), F32)
    for k in range(16):
        term = nt(t_hi, w_hi[k]) + nt(t_lo, w_hi[k]) + nt(t_hi, w_lo[k])
        change = jnp.where(rowk == k, term, change)
    solved = penalty * jnp.maximum(got - change, 0.0)
    for k in range(16):
        send_b[8 * k : 8 * k + 8] = jnp.broadcast_to(solved[k : k + 1], (8, 128))
    go_b()

    gain_rows = [
        jnp.concatenate([pre[3 * i + 2, x, 31:32] for x in range(8)], axis=0) for i in range(3)
    ]
    top = [jnp.concatenate([out[i, x, 31:32] for x in range(8)], axis=0) for i in range(3)]
    on = by_tile(con_v)
    from_row = jnp.where(lax.broadcasted_iota(jnp.int32, (32, 16), 1) == owners, 1.0, 0.0).astype(BF16)
    arrived_b()
    back = jnp.concatenate([recv_b[8 * k : 8 * k + 1] for k in range(16)], axis=0)
    home = exact(from_row, back, ((1,), (0,)))
    home = jnp.where(is_first, home, rolled(home)) * on
    first = lane8 < 64
    value = jnp.concatenate(
        [
            jnp.where(first, home[0:8], rolled(home[8:16])),
            jnp.where(first, home[16:24], rolled(home[24:32])),
        ],
        axis=1,
    )
    press[...] = value
    for i in range(3):
        fixed = top[i] - gain_rows[i] * value
        for x in range(8):
            out[i, x, 31:32] = fixed[x : x + 1]
    late = [
        local(15, out.at[:, :, pl.ds(24, 8)], out_hbm.at[:, :, pl.ds(24, 8)]),
        local(16, press, press_hbm),
    ]
    for c in late:
        c.start()
    for c in slices1 + cols1 + slices2 + cols2:
        c.wait_send()
    sent_a()
    sent_b()
    early.wait()
    for c in late:
        c.wait()


def hand_over(out, press, out_copy, press_copy, out_v, press_v, sem_in, sem_out):
    chunks = [(r.at[i], v.at[i], c.at[i]) for r, v, c in ((out, out_v, out_copy),) for i in range(3)]
    chunks.append((press, press_v, press_copy))
    get = [pltpu.make_async_copy(c[0], c[1], sem_in.at[k]) for k, c in enumerate(chunks)]
    put = [pltpu.make_async_copy(c[1], c[2], sem_out.at[k]) for k, c in enumerate(chunks)]
    for c in get:
        c.start()
    for g, p in zip(get, put):
        g.wait()
        p.start()
    for c in put:
        c.wait()


def solution(mesh):
    ngx, ngy = mesh.shape["gx"], mesh.shape["gy"]

    def per_device(
        disp_start, load, modulus, element_matrix, precond, approach, contact, owner, slot, influence
    ):
        vm = lambda shape, dtype=F32: pltpu.VMEM(shape, dtype)
        dma = lambda n: pltpu.SemaphoreType.DMA((n,))
        anywhere = pl.BlockSpec(memory_space=pltpu.HBM)
        results = pl.pallas_call(
            functools.partial(kernel, ngx, ngy),
            out_shape=(
                jax.ShapeDtypeStruct((3, 8, 32, 256), F32),
                jax.ShapeDtypeStruct((8, 256), F32),
            ),
            in_specs=[anywhere] * 13,
            out_specs=(anywhere, anywhere),
            scratch_shapes=[
                vm((3, 10, 32, 256)), vm((3, 10, 32, 256)),
                vm((3, 8, 32, 256)), vm((3, 8, 32, 256)), vm((9, 8, 32, 256)),
                vm((9, 32, 256)), vm((9, 32, 256)), vm((9, 32, 256)),
                vm((2, 10, COLS, 256), BF16), vm((2, 10, COLS, 256), BF16),
                vm((ROWS, 2 * COLS), BF16), vm((ROWS, 2 * COLS), BF16),
                vm((2, 2 * COLS, 128), BF16), vm((2, 2 * COLS, 128), BF16),
                vm((32, 128)), vm((32, 128)), vm((2, 3, 16, 128)),
                vm((3, 8, 32, 256)), vm((8, 256)),
                vm((24, 24)), vm((ROWS, 24), BF16), vm((24, 4 * COLS), BF16), vm((ROWS, 4 * COLS), BF16),
                vm((1, 8)), vm((4, 8), jnp.int32), vm((4, 8), jnp.int32), vm((4, 8), jnp.int32),
                vm((32, TW, TW)), vm((16, 128, 128), BF16), vm((16, 128, 128), BF16),
                vm((2, 8, 128)), vm((1, 8, 128)), vm((1, 8, 128)), vm((1, 8, 128)),
                vm((3, 2, 8, 128)), vm((3, 1, 8, 128)), vm((3, 1, 8, 128)), vm((3, 1, 8, 128)),
                vm((128, 128)), vm((128, 128)), vm((128, 128)), vm((128, 128)),
                dma(17), dma(17), dma(17), dma(16), dma(16), dma(16), dma(16),
            ],
            compiler_params=pltpu.CompilerParams(
                collective_id=0, has_side_effects=True, vmem_limit_bytes=60 * 1024 * 1024
            ),
        )(
            disp_start, load, modulus, element_matrix, precond, approach.reshape(1, 8),
            contact.T, owner.T, slot.T, influence.reshape(32, TW, TW), *tables(),
        )
        return pl.pallas_call(
            hand_over,
            out_shape=tuple(jax.ShapeDtypeStruct(r.shape, r.dtype) for r in results),
            in_specs=[anywhere] * 2,
            out_specs=(anywhere, anywhere),
            scratch_shapes=[vm((3, 8, 32, 256)), vm((8, 256)), dma(4), dma(4)],
            compiler_params=pltpu.CompilerParams(vmem_limit_bytes=60 * 1024 * 1024),
        )(*results)

    return jax.shard_map(
        per_device,
        mesh=mesh,
        in_specs=(
            P(None, "gx", None, "gy"),
            P(None, "gx", None, "gy"),
            P("gx", None, "gy"),
            P(),
            P(None, "gx", None, "gy"),
            P("gx"),
            P("gx", "gy"),
            P("gx", "gy"),
            P("gx", "gy"),
            P("gx", "gy", None, None, None, None),
        ),
        out_specs=(P(None, "gx", None, "gy"), P("gx", "gy")),
        check_vma=False,
    )
```

```python
import functools

import jax
import jax.numpy as jnp
import numpy as np
from jax import lax
from jax.experimental import pallas as pl
from jax.experimental.pallas import tpu as pltpu
from jax.sharding import PartitionSpec as P

MESH = pl.DeviceIdType.MESH
F32 = jnp.float32
BF16 = jnp.bfloat16

TW = 64
PITCH = 10
penalty = 1.5
crown_depth = 0.4
crown_shape = 0.96

ROWS, HALF, COLS = 384, 192, 112


def tables():
    row = np.arange(ROWS)
    layer, c_out, i_out = row % 16, row // 16 % 2, row // 32 % 3
    b_out, a_out = row // 96 % 2, row // 192
    source = 3 * (4 * a_out + 2 * b_out + c_out) + i_out
    col = np.arange(2 * COLS)
    a_in, inner = col // COLS, col % COLS
    main = inner < 96
    node = np.where(main, inner % 16, np.where(inner < 102, 16, np.where(inner < 108, -1, -100)))
    which = np.where(main, inner // 16, (inner - 96) % 6)
    b_in, i_in = which // 3, which % 3
    dof = np.arange(24)
    pick_rows = source[:, None] == dof[None, :]
    pick_cols = np.concatenate(
        [dof[:, None] == (3 * (4 * a_in + 2 * b_in + c) + i_in)[None, :] for c in (0, 1)], axis=1
    )
    band = np.concatenate(
        [node[None, :] - layer[:, None] + c_out[:, None] == c for c in (0, 1)], axis=1
    )
    return tuple(jnp.asarray(t.astype(np.float32), BF16) for t in (pick_rows, pick_cols, band))


def split(value):
    high = value.astype(BF16)
    return high, (value - high.astype(F32)).astype(BF16)


def mm(a, b):
    return jnp.dot(a, b, preferred_element_type=F32)


def kernel(
    ngx, ngy,
    disp, load, modulus, emat, precond, approach, contact, owner, slot, influence,
    pick_rows, pick_cols, band,
    out_hbm, press_hbm,
    u1, u2, res1, res2, pre, mod, coef0, coef1, s_hi, s_lo, g_hi, g_lo,
    ext_hi, ext_lo, ext0, ext1, tot, out, press,
    em_v, rows_v, cols_v, band_v, app_v, con_v, own_v, slot_v, infl, w_hi, w_lo,
    msg_r1, msg_l1, msg_r2, msg_l2, in_r1, in_l1, in_r2, in_l2,
    send_m, recv_m,
    local_sem, halo_send, halo_recv, m_send, m_recv,
):
    gx, gy = lax.axis_index("gx"), lax.axis_index("gy")
    up_x, down_x = lax.rem(gx + 1, ngx), lax.rem(gx + ngx - 1, ngx)
    up_y, down_y = lax.rem(gy + 1, ngy), lax.rem(gy + ngy - 1, ngy)

    def local(i, src, dst):
        return pltpu.make_async_copy(src, dst, local_sem.at[i])

    loads = [
        local(0, disp, u1.at[:, pl.ds(1, 8)]),
        local(1, modulus, mod.at[pl.ds(1, 8)]),
        local(2, emat, em_v),
        local(3, pick_rows, rows_v),
        local(4, pick_cols, cols_v),
        local(5, band, band_v),
        local(6, load, res1),
        local(7, precond, pre),
        local(8, load, res2),
        local(9, approach, app_v),
        local(10, contact, con_v),
        local(11, owner, own_v),
        local(12, slot, slot_v),
        local(13, influence, infl),
    ]
    for c in loads[:2]:
        c.start()

    barrier = pltpu.get_barrier_semaphore()

    def greet(d, carry):
        pl.semaphore_signal(barrier, inc=1, device_id=(lax.rem(gx + d, ngx), gy), device_id_type=MESH)
        return carry

    lax.fori_loop(1, ngx, greet, 0, unroll=True)
    for oy in (up_y, down_y):
        for ox in (down_x, gx, up_x):
            pl.semaphore_signal(barrier, inc=1, device_id=(ox, oy), device_id_type=MESH)

    def remote(i, src, dst, to):
        return pltpu.make_async_remote_copy(
            src_ref=src, dst_ref=dst, send_sem=halo_send.at[i], recv_sem=halo_recv.at[i],
            device_id=to, device_id_type=MESH,
        )

    pl.semaphore_wait(barrier, ngx - 1 + 6)
    slices1 = [
        remote(0, disp.at[:, pl.ds(7, 1)], u1.at[:, pl.ds(0, 1)], (up_x, gy)),
        remote(1, disp.at[:, pl.ds(0, 1)], u1.at[:, pl.ds(9, 1)], (down_x, gy)),
        remote(2, modulus.at[pl.ds(7, 1)], mod.at[pl.ds(0, 1)], (up_x, gy)),
    ]
    for c in slices1:
        c.start()
    for c in loads[2:]:
        c.start()

    lane8 = lax.broadcasted_iota(jnp.int32, (8, 128), 1)
    lane16 = lax.broadcasted_iota(jnp.int32, (16, 128), 1)
    row16 = lax.broadcasted_iota(jnp.int32, (16, 256), 0)

    def pack(n, u, carry):
        left, right = carry
        for i in range(3):
            for k in range(4):
                base = (i * 4 + k) * PITCH
                hit = lane8 == base + n
                first = u[i, n, 8 * k : 8 * k + 8, 0:128]
                last = u[i, n, 8 * k : 8 * k + 8, 128:256]
                left = jnp.where(hit, pltpu.roll(first, base + n, axis=1), left)
                right = jnp.where(hit, pltpu.roll(last, base + n + 1, axis=1), right)
        return left, right

    def pack_coef(n, carry):
        for k in range(4):
            base = k * PITCH
            last = mod[n, 8 * k : 8 * k + 8, 128:256]
            carry = jnp.where(lane8 == base + n, pltpu.roll(last, base + n + 1, axis=1), carry)
        return carry

    zero8 = jnp.zeros((8, 128), F32)
    loads[0].wait()
    left, right = lax.fori_loop(1, 9, lambda n, c: pack(n, u1, c), (zero8, zero8), unroll=True)
    loads[1].wait()
    own_coef = lax.fori_loop(1, 9, pack_coef, zero8, unroll=True)
    msg_l1[0] = left
    msg_r1[0] = right
    msg_r1[1] = own_coef

    def columns(first, msg_l, msg_r, in_l, in_r):
        copies = []
        for d, ox in ((0, up_x), (1, gx), (2, down_x)):
            copies.append(remote(first + d, msg_r, in_r.at[d], (ox, up_y)))
            copies.append(remote(first + 3 + d, msg_l, in_l.at[d], (ox, down_y)))
        return copies

    cols1 = columns(3, msg_l1, msg_r1, in_l1, in_r1)
    for c in cols1:
        c.start()


    def matrices(d):
        peer = lax.rem(gx + d, ngx)
        return pltpu.make_async_remote_copy(
            src_ref=send_m.at[peer], dst_ref=recv_m.at[gx], send_sem=m_send.at[d], recv_sem=m_recv.at[d],
            device_id=(peer, gy), device_id_type=MESH,
        )

    def pack_matrices(k, carry):
        send_m[k] = jnp.concatenate([infl[2 * k], infl[2 * k + 1]], axis=1)
        return carry

    loads[13].wait()
    lax.fori_loop(0, ngx, pack_matrices, 0, unroll=True)
    own_matrices = pltpu.make_async_copy(send_m.at[gx], recv_m.at[gx], m_send.at[0])
    own_matrices.start()
    for d in (1, 15, 4, 12, 2, 14, 3, 13, 5, 11, 8, 7, 9, 6, 10):
        matrices(d).start()

    for i in (2, 3, 4, 5):
        loads[i].wait()
    for part, dst in zip(split(em_v[...]), (g_hi, g_lo)):
        wide = mm(mm(rows_v[...], part).astype(BF16), cols_v[...])
        dst[...] = (
            wide[:, : 2 * COLS] * band_v[:, : 2 * COLS].astype(F32)
            + wide[:, 2 * COLS :] * band_v[:, 2 * COLS :].astype(F32)
        ).astype(BF16)

    inside = (lax.broadcasted_iota(jnp.int32, (32, 256), 0) < 31) & (
        lax.broadcasted_iota(jnp.int32, (32, 256), 1) < 255
    )
    low_x = jnp.where(gx > 0, 1.0, 0.0).astype(F32)
    high_x = jnp.where(gx < ngx - 1, 1.0, 0.0).astype(F32)
    low_y = jnp.where(gy > 0, 1.0, 0.0).astype(F32)
    high_y = jnp.where(gy < ngy - 1, 1.0, 0.0).astype(F32)

    def set_coef(e, gain):
        value = jnp.where(inside, mod[e] * gain, 0.0)
        coef0[e] = value
        coef1[e] = pltpu.roll(value, 1, axis=0)

    def some_coef(e, carry):
        set_coef(e, jnp.where(e == 8, high_x, 1.0))
        return carry

    lax.fori_loop(1, 9, some_coef, 0, unroll=True)

    def operand(n, u):
        edge = [jnp.zeros((16, 256), F32), jnp.zeros((16, 256), F32)]
        for i in range(3):
            here = u[i, n]
            for b in range(2):
                value = here if b == 0 else pltpu.roll(here, 255, axis=1)
                j = b * 3 + i
                high, low = split(value)
                for g in range(2):
                    s_hi[g, n, 16 * j : 16 * j + 16] = high[16 * g : 16 * g + 16]
                    s_lo[g, n, 16 * j : 16 * j + 16] = low[16 * g : 16 * g + 16]
                edge[0] = jnp.where(row16 == j, value[16:17], edge[0])
                edge[1] = jnp.where(row16 == 6 + j, value[15:16], edge[1])
        for g in range(2):
            high, low = split(edge[g])
            s_hi[g, n, 96:112] = high
            s_lo[g, n, 96:112] = low

    def all_operands(u):
        def one(n, carry):
            operand(n, u)
            return carry

        lax.fori_loop(1, 9, one, 0, unroll=True)

    def product(sh, sl, start, size):
        gh, gl = g_hi[start : start + size], g_lo[start : start + size]
        return mm(gh, sh) + mm(gl, sh) + mm(gh, sl)

    def elements(e, g, sides, res):
        zs = slice(16 * g, 16 * g + 16)
        sh = s_hi[g, pl.ds(e, 2)].reshape(2 * COLS, 256)
        sl = s_lo[g, pl.ds(e, 2)].reshape(2 * COLS, 256)
        c0, c1 = coef0[e, zs], coef1[e, zs]
        r = product(sh, sl, HALF * sides[0], HALF * len(sides))
        for k, a in enumerate(sides):
            for i in range(3):
                parts = []
                for b in range(2):
                    at = ((k * 2 + b) * 3 + i) * 32
                    parts.append(r[at : at + 16] * c0 + r[at + 16 : at + 32] * c1)
                x = e - 1 + a
                res[i, x, zs] = res[i, x, zs] - (parts[0] + pltpu.roll(parts[1], 1, axis=1))

    def interior(g, res):
        def one(e, carry):
            elements(e, g, (0, 1), res)
            return carry

        lax.fori_loop(1, 8, one, 0, unroll=True)

    starts = [k * PITCH for k in range(12)]
    at_low = functools.reduce(jnp.logical_or, [lane8 == s for s in starts])
    at_high = functools.reduce(jnp.logical_or, [lane8 == s + 9 for s in starts])

    def merged(below, here, above):
        value = jnp.where(at_low, pltpu.roll(below, 120, axis=1), here)
        return jnp.where(at_high, pltpu.roll(above, 8, axis=1), value)

    def both(left, right, k):
        return jnp.where(
            lane8 < 64,
            pltpu.roll(left, (128 - k * PITCH) % 128, axis=1),
            pltpu.roll(right, (192 - k * PITCH) % 128, axis=1),
        )

    def ends(left, right, in_l, in_r):
        beyond_low = merged(in_r[0, 0], in_r[1, 0], in_r[2, 0])
        beyond_high = merged(in_l[0, 0], in_l[1, 0], in_l[2, 0])
        rowm = lax.broadcasted_iota(jnp.int32, (16, 128), 0)
        for b, (lo, hi) in enumerate(((beyond_low, right), (left, beyond_high))):
            for i in range(3):
                j = b * 3 + i
                here = jnp.concatenate([both(lo, hi, i * 4 + k) for k in range(4)], axis=0)
                for a in range(2):
                    value = here if a == 0 else pltpu.roll(here, 127, axis=1)
                    high, low = split(value)
                    for g in range(2):
                        at = a * COLS + 16 * j
                        ext_hi[g, at : at + 16] = high[16 * g : 16 * g + 16]
                        ext_lo[g, at : at + 16] = low[16 * g : 16 * g + 16]
                    for g, (row, source) in enumerate(((j, 16), (6 + j, 15))):
                        tot[g, a] = jnp.where(rowm == row, value[source : source + 1], 0.0 if j == 0 else tot[g, a])
        for a in range(2):
            for g in range(2):
                high, low = split(tot[g, a])
                at = a * COLS + 96
                ext_hi[g, at : at + 16] = high
                ext_lo[g, at : at + 16] = low

    def end_coef(own_coef):
        beyond = merged(in_r1[0, 1], in_r1[1, 1], in_r1[2, 1])
        gain = jnp.where(lane8 < 9, low_y, jnp.where((lane8 >= 64) & (lane8 < 73), high_y, 0.0))
        gain = jnp.where((lane8 == 0) | (lane8 == 64), gain * low_x, gain)
        gain = jnp.where((lane8 == 8) | (lane8 == 72), gain * high_x, gain)
        value = jnp.concatenate([both(beyond, own_coef, k) * gain for k in range(4)], axis=0)
        value = jnp.where(lax.broadcasted_iota(jnp.int32, (32, 128), 0) < 31, value, 0.0)
        ext0[...] = value
        ext1[...] = pltpu.roll(value, 1, axis=0)

    def end_elements(g):
        zs = slice(16 * g, 16 * g + 16)
        r = product(ext_hi[g], ext_lo[g], 0, ROWS)
        c0, c1 = ext0[zs], ext1[zs]
        for i in range(3):
            parts = []
            for a in range(2):
                at_b0, at_b1 = (a * 6 + i) * 32, (a * 6 + 3 + i) * 32
                picked = jnp.where(lane16 < 64, r[at_b1 : at_b1 + 16], r[at_b0 : at_b0 + 16])
                shifted = jnp.where(lane16 < 64, r[at_b1 + 16 : at_b1 + 32], r[at_b0 + 16 : at_b0 + 32])
                parts.append(picked * c0 + shifted * c1)
            tot[g, i] = parts[0] + pltpu.roll(parts[1], 1, axis=1)

    def update(g, x, res, u, store):
        zs = slice(16 * g, 16 * g + 16)
        resid = []
        for i in range(3):
            sides = tot[g, i]
            low = jnp.where(lane16 == 0, pltpu.roll(sides, 127 - x, axis=1), 0.0)
            high = jnp.where(lane16 == 127, pltpu.roll(sides, 62 - x, axis=1), 0.0)
            resid.append(res[i, x, zs] - jnp.concatenate([low, high], axis=1))
        for i in range(3):
            value = u[i, x + 1, zs]
            for j in range(3):
                value = value + pre[3 * i + j, x, zs] * resid[j]
            store(i, x, zs, value)

    def update_all(g, res, u, store):
        def one(x, carry):
            update(g, x, res, u, store)
            return carry

        lax.fori_loop(0, 8, one, 0, unroll=True)

    all_operands(u1)
    loads[6].wait()
    for g in (1, 0):
        interior(g, res1)
    for c in slices1:
        c.wait_recv()
    set_coef(0, low_x)
    operand(0, u1)
    operand(9, u1)
    for g in (1, 0):
        elements(0, g, (1,), res1)
        elements(8, g, (0,), res1)
    left, right = pack(9, u1, pack(0, u1, (msg_l1[0], msg_r1[0])))
    own_coef = pack_coef(0, msg_r1[1])
    for c in cols1:
        c.wait_recv()
    ends(left, right, in_l1, in_r1)
    end_coef(own_coef)
    for g in (1, 0):
        end_elements(g)

    def store_u2(i, x, zs, value):
        u2[i, x + 1, zs] = value

    loads[7].wait()
    for g in (1, 0):
        update_all(g, res1, u1, store_u2)
    slices2 = [
        remote(9, u2.at[:, pl.ds(8, 1)], u2.at[:, pl.ds(0, 1)], (up_x, gy)),
        remote(10, u2.at[:, pl.ds(1, 1)], u2.at[:, pl.ds(9, 1)], (down_x, gy)),
    ]
    for c in slices2:
        c.start()
    left, right = lax.fori_loop(1, 9, lambda n, c: pack(n, u2, c), (zero8, zero8), unroll=True)
    msg_l2[0] = left
    msg_r2[0] = right
    cols2 = columns(11, msg_l2, msg_r2, in_l2, in_r2)
    for c in cols2:
        c.start()

    all_operands(u2)
    loads[8].wait()
    interior(1, res2)
    interior(0, res2)
    own_matrices.wait()
    for d in range(1, 16):
        matrices(d).wait_recv()

    def prepare(k, carry):
        value = recv_m[k]
        lane = lax.broadcasted_iota(jnp.int32, (TW, 128), 1)
        rows = jnp.concatenate([jnp.where(lane < TW, value, 0.0), jnp.where(lane < TW, 0.0, value)], axis=0)
        w_hi[k], w_lo[k] = split(rows)
        return carry

    lax.fori_loop(0, ngx, prepare, 0, unroll=True)

    for c in slices2:
        c.wait_recv()
    operand(0, u2)
    operand(9, u2)
    left, right = pack(9, u2, pack(0, u2, (msg_l2[0], msg_r2[0])))
    for c in cols2:
        c.wait_recv()
    ends(left, right, in_l2, in_r2)
    elements(0, 1, (1,), res2)
    elements(8, 1, (0,), res2)
    end_elements(1)

    def store_out(i, x, zs, value):
        out[i, x, zs] = value

    update_all(1, res2, u2, store_out)

    for i in (9, 10, 11, 12):
        loads[i].wait()
    lane_a = lax.broadcasted_iota(jnp.int32, (8, 8), 1)
    diag = lane_a == lax.broadcasted_iota(jnp.int32, (8, 8), 0)

    def upright(row):
        return jnp.sum(jnp.where(diag, jnp.broadcast_to(row, (8, 8)), 0.0), axis=1, keepdims=True)

    gaps = upright(app_v[...])
    y_at = (gy * 256 + lax.broadcasted_iota(jnp.int32, (1, 256), 1)).astype(F32)
    spread = (y_at + 0.5) / (256.0 * ngy) * 2.0 - 1.0
    crown = -crown_depth * jnp.log(1.0 - crown_shape * spread * spread)
    surface = jnp.concatenate([out[2, x, 31:32] for x in range(8)], axis=0)
    pen = gaps - crown - surface

    def by_tile(ref):
        value = ref[...].astype(F32)
        return jnp.concatenate([upright(value[t : t + 1]) for t in range(4)], axis=0)

    owners = by_tile(own_v).astype(jnp.int32)
    slots = by_tile(slot_v)
    lane32 = lax.broadcasted_iota(jnp.int32, (32, 128), 1)
    is_first = slots == 0

    def rolled(v):
        return pltpu.roll(v, 64, axis=1)

    halves = [pen[:, :128], pen[:, 128:]]
    tiles = jnp.concatenate([halves[0], rolled(halves[0]), halves[1], rolled(halves[1])], axis=0)
    tiles = jnp.where(lane32 < 64, tiles, 0.0)
    tiles = jnp.where(is_first, tiles, rolled(tiles))

    def exact(one_hot, value, dims):
        high, rest = split(value)
        mid, low = split(value - high.astype(F32))
        total = None
        for part in (low, mid, high):
            term = lax.dot_general(one_hot, part, (dims, ((), ())), preferred_element_type=F32)
            total = term if total is None else total + term
        return total

    to_owner = jnp.where(lax.broadcasted_iota(jnp.int32, (32, 16), 1) == owners, 1.0, 0.0).astype(BF16)
    got = exact(to_owner, tiles, ((0,), (0,)))

    trial = penalty * jnp.maximum(got, 0.0)
    t_hi, t_lo = split(trial)
    rowk = lax.broadcasted_iota(jnp.int32, (16, 128), 0)

    def nt(a, b):
        return lax.dot_general(a, b, (((1,), (1,)), ((), ())), preferred_element_type=F32)

    change = jnp.zeros((16, 128), F32)
    for k in range(16):
        term = nt(t_hi, w_hi[k]) + nt(t_lo, w_hi[k]) + nt(t_hi, w_lo[k])
        change = jnp.where(rowk == k, term, change)
    solved = penalty * jnp.maximum(got - change, 0.0)
    elements(0, 0, (1,), res2)
    elements(8, 0, (0,), res2)
    end_elements(0)
    update_all(0, res2, u2, store_out)
    early = local(14, out.at[:, :, pl.ds(0, 24)], out_hbm.at[:, :, pl.ds(0, 24)])
    early.start()


    gain_rows = [
        jnp.concatenate([pre[3 * i + 2, x, 31:32] for x in range(8)], axis=0) for i in range(3)
    ]
    top = [jnp.concatenate([out[i, x, 31:32] for x in range(8)], axis=0) for i in range(3)]
    on = by_tile(con_v)
    home = exact(to_owner, solved, ((1,), (0,)))
    home = jnp.where(is_first, home, rolled(home)) * on
    first = lane8 < 64
    value = jnp.concatenate(
        [
            jnp.where(first, home[0:8], rolled(home[8:16])),
            jnp.where(first, home[16:24], rolled(home[24:32])),
        ],
        axis=1,
    )
    press[...] = value
    for i in range(3):
        fixed = top[i] - gain_rows[i] * value
        for x in range(8):
            out[i, x, 31:32] = fixed[x : x + 1]
    late = [
        local(15, out.at[:, :, pl.ds(24, 8)], out_hbm.at[:, :, pl.ds(24, 8)]),
        local(16, press, press_hbm),
    ]
    for c in late:
        c.start()
    for c in slices1 + cols1 + slices2 + cols2:
        c.wait_send()
    for d in range(1, 16):
        matrices(d).wait_send()
    early.wait()
    for c in late:
        c.wait()


def hand_over(out, press, out_copy, press_copy, out_v, press_v, sem_in, sem_out):
    chunks = [(r.at[i], v.at[i], c.at[i]) for r, v, c in ((out, out_v, out_copy),) for i in range(3)]
    chunks.append((press, press_v, press_copy))
    get = [pltpu.make_async_copy(c[0], c[1], sem_in.at[k]) for k, c in enumerate(chunks)]
    put = [pltpu.make_async_copy(c[1], c[2], sem_out.at[k]) for k, c in enumerate(chunks)]
    for c in get:
        c.start()
    for g, p in zip(get, put):
        g.wait()
        p.start()
    for c in put:
        c.wait()


def solution(mesh):
    ngx, ngy = mesh.shape["gx"], mesh.shape["gy"]

    def per_device(
        disp_start, load, modulus, element_matrix, precond, approach, contact, owner, slot, influence
    ):
        vm = lambda shape, dtype=F32: pltpu.VMEM(shape, dtype)
        dma = lambda n: pltpu.SemaphoreType.DMA((n,))
        anywhere = pl.BlockSpec(memory_space=pltpu.HBM)
        results = pl.pallas_call(
            functools.partial(kernel, ngx, ngy),
            out_shape=(
                jax.ShapeDtypeStruct((3, 8, 32, 256), F32),
                jax.ShapeDtypeStruct((8, 256), F32),
            ),
            in_specs=[anywhere] * 13,
            out_specs=(anywhere, anywhere),
            scratch_shapes=[
                vm((3, 10, 32, 256)), vm((3, 10, 32, 256)),
                vm((3, 8, 32, 256)), vm((3, 8, 32, 256)), vm((9, 8, 32, 256)),
                vm((9, 32, 256)), vm((9, 32, 256)), vm((9, 32, 256)),
                vm((2, 10, COLS, 256), BF16), vm((2, 10, COLS, 256), BF16),
                vm((ROWS, 2 * COLS), BF16), vm((ROWS, 2 * COLS), BF16),
                vm((2, 2 * COLS, 128), BF16), vm((2, 2 * COLS, 128), BF16),
                vm((32, 128)), vm((32, 128)), vm((2, 3, 16, 128)),
                vm((3, 8, 32, 256)), vm((8, 256)),
                vm((24, 24)), vm((ROWS, 24), BF16), vm((24, 4 * COLS), BF16), vm((ROWS, 4 * COLS), BF16),
                vm((1, 8)), vm((4, 8), jnp.int32), vm((4, 8), jnp.int32), vm((4, 8), jnp.int32),
                vm((32, TW, TW)), vm((16, 128, 128), BF16), vm((16, 128, 128), BF16),
                vm((2, 8, 128)), vm((1, 8, 128)), vm((1, 8, 128)), vm((1, 8, 128)),
                vm((3, 2, 8, 128)), vm((3, 1, 8, 128)), vm((3, 1, 8, 128)), vm((3, 1, 8, 128)),
                vm((16, TW, 128)), vm((16, TW, 128)),
                dma(17), dma(17), dma(17), dma(16), dma(16),
            ],
            compiler_params=pltpu.CompilerParams(
                collective_id=0, has_side_effects=True, vmem_limit_bytes=60 * 1024 * 1024
            ),
        )(
            disp_start, load, modulus, element_matrix, precond, approach.reshape(1, 8),
            contact.T, owner.T, slot.T, influence.reshape(32, TW, TW), *tables(),
        )
        return pl.pallas_call(
            hand_over,
            out_shape=tuple(jax.ShapeDtypeStruct(r.shape, r.dtype) for r in results),
            in_specs=[anywhere] * 2,
            out_specs=(anywhere, anywhere),
            scratch_shapes=[vm((3, 8, 32, 256)), vm((8, 256)), dma(4), dma(4)],
            compiler_params=pltpu.CompilerParams(vmem_limit_bytes=60 * 1024 * 1024),
        )(*results)

    return jax.shard_map(
        per_device,
        mesh=mesh,
        in_specs=(
            P(None, "gx", None, "gy"),
            P(None, "gx", None, "gy"),
            P("gx", None, "gy"),
            P(),
            P(None, "gx", None, "gy"),
            P("gx"),
            P("gx", "gy"),
            P("gx", "gy"),
            P("gx", "gy"),
            P("gx", "gy", None, None, None, None),
        ),
        out_specs=(P(None, "gx", None, "gy"), P("gx", "gy")),
        check_vma=False,
    )
```

```python
import functools

import jax
import jax.numpy as jnp
import numpy as np
from jax import lax
from jax.experimental import pallas as pl
from jax.experimental.pallas import tpu as pltpu
from jax.sharding import PartitionSpec as P

MESH = pl.DeviceIdType.MESH
F32 = jnp.float32
BF16 = jnp.bfloat16

TW = 64
PITCH = 10
penalty = 1.5
crown_depth = 0.4
crown_shape = 0.96

ROWS, HALF, COLS = 384, 192, 112


def tables():
    row = np.arange(ROWS)
    layer, c_out, i_out = row % 16, row // 16 % 2, row // 32 % 3
    b_out, a_out = row // 96 % 2, row // 192
    source = 3 * (4 * a_out + 2 * b_out + c_out) + i_out
    col = np.arange(2 * COLS)
    a_in, inner = col // COLS, col % COLS
    main = inner < 96
    node = np.where(main, inner % 16, np.where(inner < 102, 16, np.where(inner < 108, -1, -100)))
    which = np.where(main, inner // 16, (inner - 96) % 6)
    b_in, i_in = which // 3, which % 3
    dof = np.arange(24)
    pick_rows = source[:, None] == dof[None, :]
    pick_cols = np.concatenate(
        [dof[:, None] == (3 * (4 * a_in + 2 * b_in + c) + i_in)[None, :] for c in (0, 1)], axis=1
    )
    band = np.concatenate(
        [node[None, :] - layer[:, None] + c_out[:, None] == c for c in (0, 1)], axis=1
    )
    return tuple(jnp.asarray(t.astype(np.float32), BF16) for t in (pick_rows, pick_cols, band))


def split(value):
    high = value.astype(BF16)
    return high, (value - high.astype(F32)).astype(BF16)


def mm(a, b):
    return jnp.dot(a, b, preferred_element_type=F32)


def kernel(
    ngx, ngy,
    disp, load, modulus, emat, precond, approach, contact, owner, slot, influence,
    pick_rows, pick_cols, band,
    out_hbm, press_hbm,
    u1, u2, res1, res2, pre, mod, coef0, coef1, s_hi, s_lo, g_hi, g_lo,
    ext_hi, ext_lo, ext0, ext1, tot, out, press,
    em_v, rows_v, cols_v, band_v, app_v, con_v, own_v, slot_v, infl, w_hi, w_lo,
    msg_r1, msg_l1, msg_r2, msg_l2, in_r1, in_l1, in_r2, in_l2,
    send_m, recv_m,
    local_sem, halo_send, halo_recv, m_send, m_recv,
):
    gx, gy = lax.axis_index("gx"), lax.axis_index("gy")
    up_x, down_x = lax.rem(gx + 1, ngx), lax.rem(gx + ngx - 1, ngx)
    up_y, down_y = lax.rem(gy + 1, ngy), lax.rem(gy + ngy - 1, ngy)

    def local(i, src, dst):
        return pltpu.make_async_copy(src, dst, local_sem.at[i])

    loads = [
        local(0, disp, u1.at[:, pl.ds(1, 8)]),
        local(1, modulus, mod.at[pl.ds(1, 8)]),
        local(2, emat, em_v),
        local(3, pick_rows, rows_v),
        local(4, pick_cols, cols_v),
        local(5, band, band_v),
        local(6, load, res1),
        local(7, precond, pre),
        local(8, load, res2),
        local(9, approach, app_v),
        local(10, contact, con_v),
        local(11, owner, own_v),
        local(12, slot, slot_v),
        local(13, influence, infl),
    ]
    for c in loads[:2]:
        c.start()

    barrier = pltpu.get_barrier_semaphore()

    def greet(d, carry):
        pl.semaphore_signal(barrier, inc=1, device_id=(lax.rem(gx + d, ngx), gy), device_id_type=MESH)
        return carry

    lax.fori_loop(1, ngx, greet, 0, unroll=True)
    for oy in (up_y, down_y):
        for ox in (down_x, gx, up_x):
            pl.semaphore_signal(barrier, inc=1, device_id=(ox, oy), device_id_type=MESH)

    def remote(i, src, dst, to):
        return pltpu.make_async_remote_copy(
            src_ref=src, dst_ref=dst, send_sem=halo_send.at[i], recv_sem=halo_recv.at[i],
            device_id=to, device_id_type=MESH,
        )

    pl.semaphore_wait(barrier, ngx - 1 + 6)
    slices1 = [
        remote(0, disp.at[:, pl.ds(7, 1)], u1.at[:, pl.ds(0, 1)], (up_x, gy)),
        remote(1, disp.at[:, pl.ds(0, 1)], u1.at[:, pl.ds(9, 1)], (down_x, gy)),
        remote(2, modulus.at[pl.ds(7, 1)], mod.at[pl.ds(0, 1)], (up_x, gy)),
    ]
    for c in slices1:
        c.start()
    for i in (2, 3, 4, 5, 13, 6, 9, 10, 11, 12, 7, 8):
        loads[i].start()

    lane8 = lax.broadcasted_iota(jnp.int32, (8, 128), 1)
    lane16 = lax.broadcasted_iota(jnp.int32, (16, 128), 1)
    row16 = lax.broadcasted_iota(jnp.int32, (16, 256), 0)

    def pack(n, u, carry):
        left, right = carry
        for i in range(3):
            for k in range(4):
                base = (i * 4 + k) * PITCH
                hit = lane8 == base + n
                first = u[i, n, 8 * k : 8 * k + 8, 0:128]
                last = u[i, n, 8 * k : 8 * k + 8, 128:256]
                left = jnp.where(hit, pltpu.roll(first, base + n, axis=1), left)
                right = jnp.where(hit, pltpu.roll(last, base + n + 1, axis=1), right)
        return left, right

    def pack_coef(n, carry):
        for k in range(4):
            base = k * PITCH
            last = mod[n, 8 * k : 8 * k + 8, 128:256]
            carry = jnp.where(lane8 == base + n, pltpu.roll(last, base + n + 1, axis=1), carry)
        return carry

    zero8 = jnp.zeros((8, 128), F32)
    loads[0].wait()
    left, right = lax.fori_loop(1, 9, lambda n, c: pack(n, u1, c), (zero8, zero8), unroll=True)
    loads[1].wait()
    own_coef = lax.fori_loop(1, 9, pack_coef, zero8, unroll=True)
    msg_l1[0] = left
    msg_r1[0] = right
    msg_r1[1] = own_coef

    def columns(first, msg_l, msg_r, in_l, in_r):
        copies = []
        for d, ox in ((0, up_x), (1, gx), (2, down_x)):
            copies.append(remote(first + d, msg_r, in_r.at[d], (ox, up_y)))
            copies.append(remote(first + 3 + d, msg_l, in_l.at[d], (ox, down_y)))
        return copies

    cols1 = columns(3, msg_l1, msg_r1, in_l1, in_r1)
    for c in cols1:
        c.start()


    def matrices(d):
        peer = lax.rem(gx + d, ngx)
        return pltpu.make_async_remote_copy(
            src_ref=send_m.at[peer], dst_ref=recv_m.at[gx], send_sem=m_send.at[d], recv_sem=m_recv.at[d],
            device_id=(peer, gy), device_id_type=MESH,
        )

    def pack_matrices(k, carry):
        send_m[k] = jnp.concatenate([infl[2 * k], infl[2 * k + 1]], axis=1)
        return carry

    for i in (2, 3, 4, 5):
        loads[i].wait()
    for part, dst in zip(split(em_v[...]), (g_hi, g_lo)):
        wide = mm(mm(rows_v[...], part).astype(BF16), cols_v[...])
        dst[...] = (
            wide[:, : 2 * COLS] * band_v[:, : 2 * COLS].astype(F32)
            + wide[:, 2 * COLS :] * band_v[:, 2 * COLS :].astype(F32)
        ).astype(BF16)

    inside = (lax.broadcasted_iota(jnp.int32, (32, 256), 0) < 31) & (
        lax.broadcasted_iota(jnp.int32, (32, 256), 1) < 255
    )
    low_x = jnp.where(gx > 0, 1.0, 0.0).astype(F32)
    high_x = jnp.where(gx < ngx - 1, 1.0, 0.0).astype(F32)
    low_y = jnp.where(gy > 0, 1.0, 0.0).astype(F32)
    high_y = jnp.where(gy < ngy - 1, 1.0, 0.0).astype(F32)

    def set_coef(e, gain):
        value = jnp.where(inside, mod[e] * gain, 0.0)
        coef0[e] = value
        coef1[e] = pltpu.roll(value, 1, axis=0)

    def some_coef(e, carry):
        set_coef(e, jnp.where(e == 8, high_x, 1.0))
        return carry

    lax.fori_loop(1, 9, some_coef, 0, unroll=True)

    def operand(n, u):
        edge = [jnp.zeros((16, 256), F32), jnp.zeros((16, 256), F32)]
        for i in range(3):
            here = u[i, n]
            for b in range(2):
                value = here if b == 0 else pltpu.roll(here, 255, axis=1)
                j = b * 3 + i
                high, low = split(value)
                for g in range(2):
                    s_hi[g, n, 16 * j : 16 * j + 16] = high[16 * g : 16 * g + 16]
                    s_lo[g, n, 16 * j : 16 * j + 16] = low[16 * g : 16 * g + 16]
                edge[0] = jnp.where(row16 == j, value[16:17], edge[0])
                edge[1] = jnp.where(row16 == 6 + j, value[15:16], edge[1])
        for g in range(2):
            high, low = split(edge[g])
            s_hi[g, n, 96:112] = high
            s_lo[g, n, 96:112] = low

    def all_operands(u):
        def one(n, carry):
            operand(n, u)
            return carry

        lax.fori_loop(1, 9, one, 0, unroll=True)

    def product(sh, sl, start, size):
        gh, gl = g_hi[start : start + size], g_lo[start : start + size]
        return mm(gh, sh) + mm(gl, sh) + mm(gh, sl)

    def elements(e, g, sides, res):
        zs = slice(16 * g, 16 * g + 16)
        sh = s_hi[g, pl.ds(e, 2)].reshape(2 * COLS, 256)
        sl = s_lo[g, pl.ds(e, 2)].reshape(2 * COLS, 256)
        c0, c1 = coef0[e, zs], coef1[e, zs]
        r = product(sh, sl, HALF * sides[0], HALF * len(sides))
        for k, a in enumerate(sides):
            for i in range(3):
                parts = []
                for b in range(2):
                    at = ((k * 2 + b) * 3 + i) * 32
                    parts.append(r[at : at + 16] * c0 + r[at + 16 : at + 32] * c1)
                x = e - 1 + a
                res[i, x, zs] = res[i, x, zs] - (parts[0] + pltpu.roll(parts[1], 1, axis=1))

    def interior(g, res):
        def one(e, carry):
            elements(e, g, (0, 1), res)
            return carry

        lax.fori_loop(1, 8, one, 0, unroll=True)

    starts = [k * PITCH for k in range(12)]
    at_low = functools.reduce(jnp.logical_or, [lane8 == s for s in starts])
    at_high = functools.reduce(jnp.logical_or, [lane8 == s + 9 for s in starts])

    def merged(below, here, above):
        value = jnp.where(at_low, pltpu.roll(below, 120, axis=1), here)
        return jnp.where(at_high, pltpu.roll(above, 8, axis=1), value)

    def both(left, right, k):
        return jnp.where(
            lane8 < 64,
            pltpu.roll(left, (128 - k * PITCH) % 128, axis=1),
            pltpu.roll(right, (192 - k * PITCH) % 128, axis=1),
        )

    def ends(left, right, in_l, in_r):
        beyond_low = merged(in_r[0, 0], in_r[1, 0], in_r[2, 0])
        beyond_high = merged(in_l[0, 0], in_l[1, 0], in_l[2, 0])
        rowm = lax.broadcasted_iota(jnp.int32, (16, 128), 0)
        for b, (lo, hi) in enumerate(((beyond_low, right), (left, beyond_high))):
            for i in range(3):
                j = b * 3 + i
                here = jnp.concatenate([both(lo, hi, i * 4 + k) for k in range(4)], axis=0)
                for a in range(2):
                    value = here if a == 0 else pltpu.roll(here, 127, axis=1)
                    high, low = split(value)
                    for g in range(2):
                        at = a * COLS + 16 * j
                        ext_hi[g, at : at + 16] = high[16 * g : 16 * g + 16]
                        ext_lo[g, at : at + 16] = low[16 * g : 16 * g + 16]
                    for g, (row, source) in enumerate(((j, 16), (6 + j, 15))):
                        tot[g, a] = jnp.where(rowm == row, value[source : source + 1], 0.0 if j == 0 else tot[g, a])
        for a in range(2):
            for g in range(2):
                high, low = split(tot[g, a])
                at = a * COLS + 96
                ext_hi[g, at : at + 16] = high
                ext_lo[g, at : at + 16] = low

    def end_coef(own_coef):
        beyond = merged(in_r1[0, 1], in_r1[1, 1], in_r1[2, 1])
        gain = jnp.where(lane8 < 9, low_y, jnp.where((lane8 >= 64) & (lane8 < 73), high_y, 0.0))
        gain = jnp.where((lane8 == 0) | (lane8 == 64), gain * low_x, gain)
        gain = jnp.where((lane8 == 8) | (lane8 == 72), gain * high_x, gain)
        value = jnp.concatenate([both(beyond, own_coef, k) * gain for k in range(4)], axis=0)
        value = jnp.where(lax.broadcasted_iota(jnp.int32, (32, 128), 0) < 31, value, 0.0)
        ext0[...] = value
        ext1[...] = pltpu.roll(value, 1, axis=0)

    def end_elements(g):
        zs = slice(16 * g, 16 * g + 16)
        r = product(ext_hi[g], ext_lo[g], 0, ROWS)
        c0, c1 = ext0[zs], ext1[zs]
        for i in range(3):
            parts = []
            for a in range(2):
                at_b0, at_b1 = (a * 6 + i) * 32, (a * 6 + 3 + i) * 32
                picked = jnp.where(lane16 < 64, r[at_b1 : at_b1 + 16], r[at_b0 : at_b0 + 16])
                shifted = jnp.where(lane16 < 64, r[at_b1 + 16 : at_b1 + 32], r[at_b0 + 16 : at_b0 + 32])
                parts.append(picked * c0 + shifted * c1)
            tot[g, i] = parts[0] + pltpu.roll(parts[1], 1, axis=1)

    def update(g, x, res, u, store):
        zs = slice(16 * g, 16 * g + 16)
        resid = []
        for i in range(3):
            sides = tot[g, i]
            low = jnp.where(lane16 == 0, pltpu.roll(sides, 127 - x, axis=1), 0.0)
            high = jnp.where(lane16 == 127, pltpu.roll(sides, 62 - x, axis=1), 0.0)
            resid.append(res[i, x, zs] - jnp.concatenate([low, high], axis=1))
        for i in range(3):
            value = u[i, x + 1, zs]
            for j in range(3):
                value = value + pre[3 * i + j, x, zs] * resid[j]
            store(i, x, zs, value)

    def update_all(g, res, u, store):
        def one(x, carry):
            update(g, x, res, u, store)
            return carry

        lax.fori_loop(0, 8, one, 0, unroll=True)

    all_operands(u1)
    loads[6].wait()
    interior(1, res1)
    interior(0, res1)
    loads[13].wait()
    lax.fori_loop(0, ngx, pack_matrices, 0, unroll=True)
    own_matrices = pltpu.make_async_copy(send_m.at[gx], recv_m.at[gx], m_send.at[0])
    own_matrices.start()
    for d in (1, 15, 4, 12, 2, 14, 3, 13, 5, 11, 8, 7, 9, 6, 10):
        matrices(d).start()

    for c in slices1:
        c.wait_recv()
    set_coef(0, low_x)
    operand(0, u1)
    operand(9, u1)
    for g in (1, 0):
        elements(0, g, (1,), res1)
        elements(8, g, (0,), res1)
    left, right = pack(9, u1, pack(0, u1, (msg_l1[0], msg_r1[0])))
    own_coef = pack_coef(0, msg_r1[1])
    for c in cols1:
        c.wait_recv()
    ends(left, right, in_l1, in_r1)
    end_coef(own_coef)
    for g in (1, 0):
        end_elements(g)

    def store_u2(i, x, zs, value):
        u2[i, x + 1, zs] = value

    loads[7].wait()
    for x in (0, 7):
        for g in (1, 0):
            update(g, x, res1, u1, store_u2)
    slices2 = [
        remote(9, u2.at[:, pl.ds(8, 1)], u2.at[:, pl.ds(0, 1)], (up_x, gy)),
        remote(10, u2.at[:, pl.ds(1, 1)], u2.at[:, pl.ds(9, 1)], (down_x, gy)),
    ]
    for c in slices2:
        c.start()
    for x in range(1, 7):
        for g in (1, 0):
            update(g, x, res1, u1, store_u2)
    left, right = lax.fori_loop(1, 9, lambda n, c: pack(n, u2, c), (zero8, zero8), unroll=True)
    msg_l2[0] = left
    msg_r2[0] = right
    cols2 = columns(11, msg_l2, msg_r2, in_l2, in_r2)
    for c in cols2:
        c.start()

    all_operands(u2)
    loads[8].wait()
    interior(1, res2)
    interior(0, res2)
    for c in slices2:
        c.wait_recv()
    operand(0, u2)
    operand(9, u2)
    left, right = pack(9, u2, pack(0, u2, (msg_l2[0], msg_r2[0])))
    for c in cols2:
        c.wait_recv()
    ends(left, right, in_l2, in_r2)
    def store_out(i, x, zs, value):
        out[i, x, zs] = value

    early = []
    for g in (0, 1):
        elements(0, g, (1,), res2)
        elements(8, g, (0,), res2)
        end_elements(g)
        update_all(g, res2, u2, store_out)
        zs = pl.ds(16 * g, 16 - 8 * g)
        early.append(local(14 + g, out.at[:, :, zs], out_hbm.at[:, :, zs]))
        early[g].start()

    own_matrices.wait()
    for d in range(1, 16):
        matrices(d).wait_recv()

    def prepare(k, carry):
        value = recv_m[k]
        lane = lax.broadcasted_iota(jnp.int32, (TW, 128), 1)
        rows = jnp.concatenate([jnp.where(lane < TW, value, 0.0), jnp.where(lane < TW, 0.0, value)], axis=0)
        w_hi[k], w_lo[k] = split(rows)
        return carry

    lax.fori_loop(0, ngx, prepare, 0, unroll=True)

    for i in (9, 10, 11, 12):
        loads[i].wait()
    lane_a = lax.broadcasted_iota(jnp.int32, (8, 8), 1)
    diag = lane_a == lax.broadcasted_iota(jnp.int32, (8, 8), 0)

    def upright(row):
        return jnp.sum(jnp.where(diag, jnp.broadcast_to(row, (8, 8)), 0.0), axis=1, keepdims=True)

    gaps = upright(app_v[...])
    y_at = (gy * 256 + lax.broadcasted_iota(jnp.int32, (1, 256), 1)).astype(F32)
    spread = (y_at + 0.5) / (256.0 * ngy) * 2.0 - 1.0
    crown = -crown_depth * jnp.log(1.0 - crown_shape * spread * spread)
    surface = jnp.concatenate([out[2, x, 31:32] for x in range(8)], axis=0)
    pen = gaps - crown - surface

    def by_tile(ref):
        value = ref[...].astype(F32)
        return jnp.concatenate([upright(value[t : t + 1]) for t in range(4)], axis=0)

    owners = by_tile(own_v).astype(jnp.int32)
    slots = by_tile(slot_v)
    lane32 = lax.broadcasted_iota(jnp.int32, (32, 128), 1)
    is_first = slots == 0

    def rolled(v):
        return pltpu.roll(v, 64, axis=1)

    halves = [pen[:, :128], pen[:, 128:]]
    tiles = jnp.concatenate([halves[0], rolled(halves[0]), halves[1], rolled(halves[1])], axis=0)
    tiles = jnp.where(lane32 < 64, tiles, 0.0)
    tiles = jnp.where(is_first, tiles, rolled(tiles))

    def exact(one_hot, value, dims):
        high, rest = split(value)
        mid, low = split(value - high.astype(F32))
        total = None
        for part in (low, mid, high):
            term = lax.dot_general(one_hot, part, (dims, ((), ())), preferred_element_type=F32)
            total = term if total is None else total + term
        return total

    to_owner = jnp.where(lax.broadcasted_iota(jnp.int32, (32, 16), 1) == owners, 1.0, 0.0).astype(BF16)
    got = exact(to_owner, tiles, ((0,), (0,)))

    trial = penalty * jnp.maximum(got, 0.0)
    t_hi, t_lo = split(trial)
    rowk = lax.broadcasted_iota(jnp.int32, (16, 128), 0)

    def nt(a, b):
        return lax.dot_general(a, b, (((1,), (1,)), ((), ())), preferred_element_type=F32)

    change = jnp.zeros((16, 128), F32)
    for k in range(16):
        term = nt(t_hi, w_hi[k]) + nt(t_lo, w_hi[k]) + nt(t_hi, w_lo[k])
        change = jnp.where(rowk == k, term, change)
    solved = penalty * jnp.maximum(got - change, 0.0)
    gain_rows = [
        jnp.concatenate([pre[3 * i + 2, x, 31:32] for x in range(8)], axis=0) for i in range(3)
    ]
    top = [jnp.concatenate([out[i, x, 31:32] for x in range(8)], axis=0) for i in range(3)]
    on = by_tile(con_v)
    home = exact(to_owner, solved, ((1,), (0,)))
    home = jnp.where(is_first, home, rolled(home)) * on
    first = lane8 < 64
    value = jnp.concatenate(
        [
            jnp.where(first, home[0:8], rolled(home[8:16])),
            jnp.where(first, home[16:24], rolled(home[24:32])),
        ],
        axis=1,
    )
    press[...] = value
    for i in range(3):
        fixed = top[i] - gain_rows[i] * value
        for x in range(8):
            out[i, x, 31:32] = fixed[x : x + 1]
    late = [
        local(16, out.at[:, :, pl.ds(24, 8)], out_hbm.at[:, :, pl.ds(24, 8)]),
        local(17, press, press_hbm),
    ]
    for c in late:
        c.start()
    for c in slices1 + cols1 + slices2 + cols2:
        c.wait_send()
    for d in range(1, 16):
        matrices(d).wait_send()
    for c in early + late:
        c.wait()


def hand_over(out, press, out_copy, press_copy, out_v, press_v, sem_in, sem_out):
    chunks = [(r.at[i], v.at[i], c.at[i]) for r, v, c in ((out, out_v, out_copy),) for i in range(3)]
    chunks.append((press, press_v, press_copy))
    get = [pltpu.make_async_copy(c[0], c[1], sem_in.at[k]) for k, c in enumerate(chunks)]
    put = [pltpu.make_async_copy(c[1], c[2], sem_out.at[k]) for k, c in enumerate(chunks)]
    for c in get:
        c.start()
    for g, p in zip(get, put):
        g.wait()
        p.start()
    for c in put:
        c.wait()


def solution(mesh):
    ngx, ngy = mesh.shape["gx"], mesh.shape["gy"]

    def per_device(
        disp_start, load, modulus, element_matrix, precond, approach, contact, owner, slot, influence
    ):
        vm = lambda shape, dtype=F32: pltpu.VMEM(shape, dtype)
        dma = lambda n: pltpu.SemaphoreType.DMA((n,))
        anywhere = pl.BlockSpec(memory_space=pltpu.HBM)
        results = pl.pallas_call(
            functools.partial(kernel, ngx, ngy),
            out_shape=(
                jax.ShapeDtypeStruct((3, 8, 32, 256), F32),
                jax.ShapeDtypeStruct((8, 256), F32),
            ),
            in_specs=[anywhere] * 13,
            out_specs=(anywhere, anywhere),
            scratch_shapes=[
                vm((3, 10, 32, 256)), vm((3, 10, 32, 256)),
                vm((3, 8, 32, 256)), vm((3, 8, 32, 256)), vm((9, 8, 32, 256)),
                vm((9, 32, 256)), vm((9, 32, 256)), vm((9, 32, 256)),
                vm((2, 10, COLS, 256), BF16), vm((2, 10, COLS, 256), BF16),
                vm((ROWS, 2 * COLS), BF16), vm((ROWS, 2 * COLS), BF16),
                vm((2, 2 * COLS, 128), BF16), vm((2, 2 * COLS, 128), BF16),
                vm((32, 128)), vm((32, 128)), vm((2, 3, 16, 128)),
                vm((3, 8, 32, 256)), vm((8, 256)),
                vm((24, 24)), vm((ROWS, 24), BF16), vm((24, 4 * COLS), BF16), vm((ROWS, 4 * COLS), BF16),
                vm((1, 8)), vm((4, 8), jnp.int32), vm((4, 8), jnp.int32), vm((4, 8), jnp.int32),
                vm((32, TW, TW)), vm((16, 128, 128), BF16), vm((16, 128, 128), BF16),
                vm((2, 8, 128)), vm((1, 8, 128)), vm((1, 8, 128)), vm((1, 8, 128)),
                vm((3, 2, 8, 128)), vm((3, 1, 8, 128)), vm((3, 1, 8, 128)), vm((3, 1, 8, 128)),
                vm((16, TW, 128)), vm((16, TW, 128)),
                dma(18), dma(17), dma(17), dma(16), dma(16),
            ],
            compiler_params=pltpu.CompilerParams(
                collective_id=0, has_side_effects=True, vmem_limit_bytes=60 * 1024 * 1024
            ),
        )(
            disp_start, load, modulus, element_matrix, precond, approach.reshape(1, 8),
            contact.T, owner.T, slot.T, influence.reshape(32, TW, TW), *tables(),
        )
        return pl.pallas_call(
            hand_over,
            out_shape=tuple(jax.ShapeDtypeStruct(r.shape, r.dtype) for r in results),
            in_specs=[anywhere] * 2,
            out_specs=(anywhere, anywhere),
            scratch_shapes=[vm((3, 8, 32, 256)), vm((8, 256)), dma(4), dma(4)],
            compiler_params=pltpu.CompilerParams(vmem_limit_bytes=60 * 1024 * 1024),
        )(*results)

    return jax.shard_map(
        per_device,
        mesh=mesh,
        in_specs=(
            P(None, "gx", None, "gy"),
            P(None, "gx", None, "gy"),
            P("gx", None, "gy"),
            P(),
            P(None, "gx", None, "gy"),
            P("gx"),
            P("gx", "gy"),
            P("gx", "gy"),
            P("gx", "gy"),
            P("gx", "gy", None, None, None, None),
        ),
        out_specs=(P(None, "gx", None, "gy"), P("gx", "gy")),
        check_vma=False,
    )
```

```python
import functools

import jax
import jax.numpy as jnp
import numpy as np
from jax import lax
from jax.experimental import pallas as pl
from jax.experimental.pallas import tpu as pltpu
from jax.sharding import PartitionSpec as P

MESH = pl.DeviceIdType.MESH
F32 = jnp.float32
BF16 = jnp.bfloat16

TW = 64
PITCH = 10
penalty = 1.5
crown_depth = 0.4
crown_shape = 0.96

ROWS, HALF, COLS = 384, 192, 112


def tables():
    row = np.arange(ROWS)
    layer, c_out, i_out = row % 16, row // 16 % 2, row // 32 % 3
    b_out, a_out = row // 96 % 2, row // 192
    source = 3 * (4 * a_out + 2 * b_out + c_out) + i_out
    col = np.arange(2 * COLS)
    a_in, inner = col // COLS, col % COLS
    main = inner < 96
    node = np.where(main, inner % 16, np.where(inner < 102, 16, np.where(inner < 108, -1, -100)))
    which = np.where(main, inner // 16, (inner - 96) % 6)
    b_in, i_in = which // 3, which % 3
    dof = np.arange(24)
    pick_rows = source[:, None] == dof[None, :]
    pick_cols = np.concatenate(
        [dof[:, None] == (3 * (4 * a_in + 2 * b_in + c) + i_in)[None, :] for c in (0, 1)], axis=1
    )
    band = np.concatenate(
        [node[None, :] - layer[:, None] + c_out[:, None] == c for c in (0, 1)], axis=1
    )
    return tuple(jnp.asarray(t.astype(np.float32), BF16) for t in (pick_rows, pick_cols, band))


def split(value):
    high = value.astype(BF16)
    return high, (value - high.astype(F32)).astype(BF16)


def mm(a, b):
    return jnp.dot(a, b, preferred_element_type=F32)


def kernel(
    ngx, ngy,
    disp, load, modulus, emat, precond, approach, contact, owner, slot, influence,
    pick_rows, pick_cols, band,
    out_hbm, press_hbm,
    u1, u2, res1, res2, pre, mod, coef0, coef1, s_hi, s_lo, g_hi, g_lo,
    ext_hi, ext_lo, ext0, ext1, tot, out, press,
    em_v, rows_v, cols_v, band_v, app_v, con_v, own_v, slot_v, infl, w_hi, w_lo,
    msg_r1, msg_l1, msg_r2, msg_l2, in_r1, in_l1, in_r2, in_l2,
    send_m, recv_m,
    local_sem, halo_send, halo_recv, m_send, m_recv,
):
    gx, gy = lax.axis_index("gx"), lax.axis_index("gy")
    up_x, down_x = lax.rem(gx + 1, ngx), lax.rem(gx + ngx - 1, ngx)
    up_y, down_y = lax.rem(gy + 1, ngy), lax.rem(gy + ngy - 1, ngy)

    def local(i, src, dst):
        return pltpu.make_async_copy(src, dst, local_sem.at[i])

    loads = [
        local(0, disp, u1.at[:, pl.ds(1, 8)]),
        local(1, modulus, mod.at[pl.ds(1, 8)]),
        local(2, emat, em_v),
        local(3, pick_rows, rows_v),
        local(4, pick_cols, cols_v),
        local(5, band, band_v),
        local(6, load, res1),
        local(7, precond, pre),
        local(8, load, res2),
        local(9, approach, app_v),
        local(10, contact, con_v),
        local(11, owner, own_v),
        local(12, slot, slot_v),
        local(13, influence, infl),
    ]
    for c in loads[:2]:
        c.start()

    barrier = pltpu.get_barrier_semaphore()

    def greet(d, carry):
        pl.semaphore_signal(barrier, inc=1, device_id=(lax.rem(gx + d, ngx), gy), device_id_type=MESH)
        return carry

    lax.fori_loop(1, ngx, greet, 0, unroll=True)
    for oy in (up_y, down_y):
        for ox in (down_x, gx, up_x):
            pl.semaphore_signal(barrier, inc=1, device_id=(ox, oy), device_id_type=MESH)

    def remote(i, src, dst, to):
        return pltpu.make_async_remote_copy(
            src_ref=src, dst_ref=dst, send_sem=halo_send.at[i], recv_sem=halo_recv.at[i],
            device_id=to, device_id_type=MESH,
        )

    pl.semaphore_wait(barrier, ngx - 1 + 6)
    slices1 = [
        remote(0, disp.at[:, pl.ds(7, 1)], u1.at[:, pl.ds(0, 1)], (up_x, gy)),
        remote(1, disp.at[:, pl.ds(0, 1)], u1.at[:, pl.ds(9, 1)], (down_x, gy)),
        remote(2, modulus.at[pl.ds(7, 1)], mod.at[pl.ds(0, 1)], (up_x, gy)),
    ]
    for c in slices1:
        c.start()
    for i in (2, 3, 4, 5, 13, 6, 9, 10, 11, 12, 7, 8):
        loads[i].start()

    lane8 = lax.broadcasted_iota(jnp.int32, (8, 128), 1)
    lane16 = lax.broadcasted_iota(jnp.int32, (16, 128), 1)
    row16 = lax.broadcasted_iota(jnp.int32, (16, 256), 0)

    def pack(n, u, carry):
        left, right = carry
        for i in range(3):
            for k in range(4):
                base = (i * 4 + k) * PITCH
                hit = lane8 == base + n
                first = u[i, n, 8 * k : 8 * k + 8, 0:128]
                last = u[i, n, 8 * k : 8 * k + 8, 128:256]
                left = jnp.where(hit, pltpu.roll(first, base + n, axis=1), left)
                right = jnp.where(hit, pltpu.roll(last, base + n + 1, axis=1), right)
        return left, right

    def pack_coef(n, carry):
        for k in range(4):
            base = k * PITCH
            last = mod[n, 8 * k : 8 * k + 8, 128:256]
            carry = jnp.where(lane8 == base + n, pltpu.roll(last, base + n + 1, axis=1), carry)
        return carry

    zero8 = jnp.zeros((8, 128), F32)
    loads[0].wait()
    left, right = lax.fori_loop(1, 9, lambda n, c: pack(n, u1, c), (zero8, zero8), unroll=True)
    loads[1].wait()
    own_coef = lax.fori_loop(1, 9, pack_coef, zero8, unroll=True)
    msg_l1[0] = left
    msg_r1[0] = right
    msg_r1[1] = own_coef

    def columns(first, msg_l, msg_r, in_l, in_r):
        copies = []
        for d, ox in ((0, up_x), (1, gx), (2, down_x)):
            copies.append(remote(first + d, msg_r, in_r.at[d], (ox, up_y)))
            copies.append(remote(first + 3 + d, msg_l, in_l.at[d], (ox, down_y)))
        return copies

    cols1 = columns(3, msg_l1, msg_r1, in_l1, in_r1)
    for c in cols1:
        c.start()


    def matrices(d):
        peer = lax.rem(gx + d, ngx)
        return pltpu.make_async_remote_copy(
            src_ref=send_m.at[peer], dst_ref=recv_m.at[gx], send_sem=m_send.at[d], recv_sem=m_recv.at[d],
            device_id=(peer, gy), device_id_type=MESH,
        )

    def pack_matrices(k, carry):
        send_m[k] = jnp.concatenate([infl[2 * k], infl[2 * k + 1]], axis=1)
        return carry

    for i in (2, 3, 4, 5):
        loads[i].wait()
    for part, dst in zip(split(em_v[...]), (g_hi, g_lo)):
        wide = mm(mm(rows_v[...], part).astype(BF16), cols_v[...])
        dst[...] = (
            wide[:, : 2 * COLS] * band_v[:, : 2 * COLS].astype(F32)
            + wide[:, 2 * COLS :] * band_v[:, 2 * COLS :].astype(F32)
        ).astype(BF16)

    inside = (lax.broadcasted_iota(jnp.int32, (32, 256), 0) < 31) & (
        lax.broadcasted_iota(jnp.int32, (32, 256), 1) < 255
    )
    low_x = jnp.where(gx > 0, 1.0, 0.0).astype(F32)
    high_x = jnp.where(gx < ngx - 1, 1.0, 0.0).astype(F32)
    low_y = jnp.where(gy > 0, 1.0, 0.0).astype(F32)
    high_y = jnp.where(gy < ngy - 1, 1.0, 0.0).astype(F32)

    def set_coef(e, gain):
        value = jnp.where(inside, mod[e] * gain, 0.0)
        coef0[e] = value
        coef1[e] = pltpu.roll(value, 1, axis=0)

    def some_coef(e, carry):
        set_coef(e, jnp.where(e == 8, high_x, 1.0))
        return carry

    lax.fori_loop(1, 9, some_coef, 0, unroll=True)

    def operand(n, u):
        edge = [jnp.zeros((16, 256), F32), jnp.zeros((16, 256), F32)]
        for i in range(3):
            here = u[i, n]
            for b in range(2):
                value = here if b == 0 else pltpu.roll(here, 255, axis=1)
                j = b * 3 + i
                high, low = split(value)
                for g in range(2):
                    s_hi[g, n, 16 * j : 16 * j + 16] = high[16 * g : 16 * g + 16]
                    s_lo[g, n, 16 * j : 16 * j + 16] = low[16 * g : 16 * g + 16]
                edge[0] = jnp.where(row16 == j, value[16:17], edge[0])
                edge[1] = jnp.where(row16 == 6 + j, value[15:16], edge[1])
        for g in range(2):
            high, low = split(edge[g])
            s_hi[g, n, 96:112] = high
            s_lo[g, n, 96:112] = low

    def all_operands(u):
        def one(n, carry):
            operand(n, u)
            return carry

        lax.fori_loop(1, 9, one, 0, unroll=True)

    def product(sh, sl, start, size):
        gh, gl = g_hi[start : start + size], g_lo[start : start + size]
        return mm(gh, sh) + mm(gl, sh) + mm(gh, sl)

    def elements(e, g, sides, res):
        zs = slice(16 * g, 16 * g + 16)
        sh = s_hi[g, pl.ds(e, 2)].reshape(2 * COLS, 256)
        sl = s_lo[g, pl.ds(e, 2)].reshape(2 * COLS, 256)
        c0, c1 = coef0[e, zs], coef1[e, zs]
        r = product(sh, sl, HALF * sides[0], HALF * len(sides))
        for k, a in enumerate(sides):
            for i in range(3):
                parts = []
                for b in range(2):
                    at = ((k * 2 + b) * 3 + i) * 32
                    parts.append(r[at : at + 16] * c0 + r[at + 16 : at + 32] * c1)
                x = e - 1 + a
                res[i, x, zs] = res[i, x, zs] - (parts[0] + pltpu.roll(parts[1], 1, axis=1))

    def interior(g, res):
        def one(e, carry):
            elements(e, g, (0, 1), res)
            return carry

        lax.fori_loop(1, 8, one, 0, unroll=True)

    starts = [k * PITCH for k in range(12)]
    at_low = functools.reduce(jnp.logical_or, [lane8 == s for s in starts])
    at_high = functools.reduce(jnp.logical_or, [lane8 == s + 9 for s in starts])

    def merged(below, here, above):
        value = jnp.where(at_low, pltpu.roll(below, 120, axis=1), here)
        return jnp.where(at_high, pltpu.roll(above, 8, axis=1), value)

    def both(left, right, k):
        return jnp.where(
            lane8 < 64,
            pltpu.roll(left, (128 - k * PITCH) % 128, axis=1),
            pltpu.roll(right, (192 - k * PITCH) % 128, axis=1),
        )

    def ends(left, right, in_l, in_r):
        beyond_low = merged(in_r[0, 0], in_r[1, 0], in_r[2, 0])
        beyond_high = merged(in_l[0, 0], in_l[1, 0], in_l[2, 0])
        rowm = lax.broadcasted_iota(jnp.int32, (16, 128), 0)
        for b, (lo, hi) in enumerate(((beyond_low, right), (left, beyond_high))):
            for i in range(3):
                j = b * 3 + i
                here = jnp.concatenate([both(lo, hi, i * 4 + k) for k in range(4)], axis=0)
                for a in range(2):
                    value = here if a == 0 else pltpu.roll(here, 127, axis=1)
                    high, low = split(value)
                    for g in range(2):
                        at = a * COLS + 16 * j
                        ext_hi[g, at : at + 16] = high[16 * g : 16 * g + 16]
                        ext_lo[g, at : at + 16] = low[16 * g : 16 * g + 16]
                    for g, (row, source) in enumerate(((j, 16), (6 + j, 15))):
                        tot[g, a] = jnp.where(rowm == row, value[source : source + 1], 0.0 if j == 0 else tot[g, a])
        for a in range(2):
            for g in range(2):
                high, low = split(tot[g, a])
                at = a * COLS + 96
                ext_hi[g, at : at + 16] = high
                ext_lo[g, at : at + 16] = low

    def end_coef(own_coef):
        beyond = merged(in_r1[0, 1], in_r1[1, 1], in_r1[2, 1])
        gain = jnp.where(lane8 < 9, low_y, jnp.where((lane8 >= 64) & (lane8 < 73), high_y, 0.0))
        gain = jnp.where((lane8 == 0) | (lane8 == 64), gain * low_x, gain)
        gain = jnp.where((lane8 == 8) | (lane8 == 72), gain * high_x, gain)
        value = jnp.concatenate([both(beyond, own_coef, k) * gain for k in range(4)], axis=0)
        value = jnp.where(lax.broadcasted_iota(jnp.int32, (32, 128), 0) < 31, value, 0.0)
        ext0[...] = value
        ext1[...] = pltpu.roll(value, 1, axis=0)

    def end_elements(g):
        zs = slice(16 * g, 16 * g + 16)
        r = product(ext_hi[g], ext_lo[g], 0, ROWS)
        c0, c1 = ext0[zs], ext1[zs]
        for i in range(3):
            parts = []
            for a in range(2):
                at_b0, at_b1 = (a * 6 + i) * 32, (a * 6 + 3 + i) * 32
                picked = jnp.where(lane16 < 64, r[at_b1 : at_b1 + 16], r[at_b0 : at_b0 + 16])
                shifted = jnp.where(lane16 < 64, r[at_b1 + 16 : at_b1 + 32], r[at_b0 + 16 : at_b0 + 32])
                parts.append(picked * c0 + shifted * c1)
            tot[g, i] = parts[0] + pltpu.roll(parts[1], 1, axis=1)

    def update(g, x, res, u, store):
        zs = slice(16 * g, 16 * g + 16)
        resid = []
        for i in range(3):
            sides = tot[g, i]
            low = jnp.where(lane16 == 0, pltpu.roll(sides, 127 - x, axis=1), 0.0)
            high = jnp.where(lane16 == 127, pltpu.roll(sides, 62 - x, axis=1), 0.0)
            resid.append(res[i, x, zs] - jnp.concatenate([low, high], axis=1))
        for i in range(3):
            value = u[i, x + 1, zs]
            for j in range(3):
                value = value + pre[3 * i + j, x, zs] * resid[j]
            store(i, x, zs, value)

    def update_all(g, res, u, store):
        def one(x, carry):
            update(g, x, res, u, store)
            return carry

        lax.fori_loop(0, 8, one, 0, unroll=True)

    all_operands(u1)
    loads[6].wait()
    interior(1, res1)
    interior(0, res1)
    loads[13].wait()
    lax.fori_loop(0, ngx, pack_matrices, 0, unroll=True)
    own_matrices = pltpu.make_async_copy(send_m.at[gx], recv_m.at[gx], m_send.at[0])
    own_matrices.start()
    for d in (10, 6, 9, 11, 7, 5, 14, 2, 8, 13, 3, 15, 1, 12, 4):
        matrices(d).start()

    for c in slices1:
        c.wait_recv()
    set_coef(0, low_x)
    operand(0, u1)
    operand(9, u1)
    for g in (1, 0):
        elements(0, g, (1,), res1)
        elements(8, g, (0,), res1)
    left, right = pack(9, u1, pack(0, u1, (msg_l1[0], msg_r1[0])))
    own_coef = pack_coef(0, msg_r1[1])
    for c in cols1:
        c.wait_recv()
    ends(left, right, in_l1, in_r1)
    end_coef(own_coef)
    for g in (1, 0):
        end_elements(g)

    def store_u2(i, x, zs, value):
        u2[i, x + 1, zs] = value

    loads[7].wait()
    for x in (0, 7):
        for g in (1, 0):
            update(g, x, res1, u1, store_u2)
    slices2 = [
        remote(9, u2.at[:, pl.ds(8, 1)], u2.at[:, pl.ds(0, 1)], (up_x, gy)),
        remote(10, u2.at[:, pl.ds(1, 1)], u2.at[:, pl.ds(9, 1)], (down_x, gy)),
    ]
    for c in slices2:
        c.start()
    for x in range(1, 7):
        for g in (1, 0):
            update(g, x, res1, u1, store_u2)
    left, right = lax.fori_loop(1, 9, lambda n, c: pack(n, u2, c), (zero8, zero8), unroll=True)
    msg_l2[0] = left
    msg_r2[0] = right
    cols2 = columns(11, msg_l2, msg_r2, in_l2, in_r2)
    for c in cols2:
        c.start()

    all_operands(u2)
    loads[8].wait()
    interior(1, res2)
    interior(0, res2)
    for c in slices2:
        c.wait_recv()
    operand(0, u2)
    operand(9, u2)
    left, right = pack(9, u2, pack(0, u2, (msg_l2[0], msg_r2[0])))
    for c in cols2:
        c.wait_recv()
    ends(left, right, in_l2, in_r2)
    def store_out(i, x, zs, value):
        out[i, x, zs] = value

    early = []
    for g in (0, 1):
        elements(0, g, (1,), res2)
        elements(8, g, (0,), res2)
        end_elements(g)
        update_all(g, res2, u2, store_out)
        zs = pl.ds(16 * g, 16 - 8 * g)
        early.append(local(14 + g, out.at[:, :, zs], out_hbm.at[:, :, zs]))
        early[g].start()

    own_matrices.wait()
    for d in range(1, 16):
        matrices(d).wait_recv()

    def prepare(k, carry):
        value = recv_m[k]
        lane = lax.broadcasted_iota(jnp.int32, (TW, 128), 1)
        rows = jnp.concatenate([jnp.where(lane < TW, value, 0.0), jnp.where(lane < TW, 0.0, value)], axis=0)
        w_hi[k], w_lo[k] = split(rows)
        return carry

    lax.fori_loop(0, ngx, prepare, 0, unroll=True)

    for i in (9, 10, 11, 12):
        loads[i].wait()
    lane_a = lax.broadcasted_iota(jnp.int32, (8, 8), 1)
    diag = lane_a == lax.broadcasted_iota(jnp.int32, (8, 8), 0)

    def upright(row):
        return jnp.sum(jnp.where(diag, jnp.broadcast_to(row, (8, 8)), 0.0), axis=1, keepdims=True)

    gaps = upright(app_v[...])
    y_at = (gy * 256 + lax.broadcasted_iota(jnp.int32, (1, 256), 1)).astype(F32)
    spread = (y_at + 0.5) / (256.0 * ngy) * 2.0 - 1.0
    crown = -crown_depth * jnp.log(1.0 - crown_shape * spread * spread)
    surface = jnp.concatenate([out[2, x, 31:32] for x in range(8)], axis=0)
    pen = gaps - crown - surface

    def by_tile(ref):
        value = ref[...].astype(F32)
        return jnp.concatenate([upright(value[t : t + 1]) for t in range(4)], axis=0)

    owners = by_tile(own_v).astype(jnp.int32)
    slots = by_tile(slot_v)
    lane32 = lax.broadcasted_iota(jnp.int32, (32, 128), 1)
    is_first = slots == 0

    def rolled(v):
        return pltpu.roll(v, 64, axis=1)

    halves = [pen[:, :128], pen[:, 128:]]
    tiles = jnp.concatenate([halves[0], rolled(halves[0]), halves[1], rolled(halves[1])], axis=0)
    tiles = jnp.where(lane32 < 64, tiles, 0.0)
    tiles = jnp.where(is_first, tiles, rolled(tiles))

    def exact(one_hot, value, dims):
        high, rest = split(value)
        mid, low = split(value - high.astype(F32))
        total = None
        for part in (low, mid, high):
            term = lax.dot_general(one_hot, part, (dims, ((), ())), preferred_element_type=F32)
            total = term if total is None else total + term
        return total

    to_owner = jnp.where(lax.broadcasted_iota(jnp.int32, (32, 16), 1) == owners, 1.0, 0.0).astype(BF16)
    got = exact(to_owner, tiles, ((0,), (0,)))

    trial = penalty * jnp.maximum(got, 0.0)
    t_hi, t_lo = split(trial)
    rowk = lax.broadcasted_iota(jnp.int32, (16, 128), 0)

    def nt(a, b):
        return lax.dot_general(a, b, (((1,), (1,)), ((), ())), preferred_element_type=F32)

    change = jnp.zeros((16, 128), F32)
    for k in range(16):
        term = nt(t_hi, w_hi[k]) + nt(t_lo, w_hi[k]) + nt(t_hi, w_lo[k])
        change = jnp.where(rowk == k, term, change)
    solved = penalty * jnp.maximum(got - change, 0.0)
    gain_rows = [
        jnp.concatenate([pre[3 * i + 2, x, 31:32] for x in range(8)], axis=0) for i in range(3)
    ]
    top = [jnp.concatenate([out[i, x, 31:32] for x in range(8)], axis=0) for i in range(3)]
    on = by_tile(con_v)
    home = exact(to_owner, solved, ((1,), (0,)))
    home = jnp.where(is_first, home, rolled(home)) * on
    first = lane8 < 64
    value = jnp.concatenate(
        [
            jnp.where(first, home[0:8], rolled(home[8:16])),
            jnp.where(first, home[16:24], rolled(home[24:32])),
        ],
        axis=1,
    )
    press[...] = value
    for i in range(3):
        fixed = top[i] - gain_rows[i] * value
        for x in range(8):
            out[i, x, 31:32] = fixed[x : x + 1]
    late = [
        local(16, out.at[:, :, pl.ds(24, 8)], out_hbm.at[:, :, pl.ds(24, 8)]),
        local(17, press, press_hbm),
    ]
    for c in late:
        c.start()
    for c in slices1 + cols1 + slices2 + cols2:
        c.wait_send()
    for d in range(1, 16):
        matrices(d).wait_send()
    for c in early + late:
        c.wait()


def hand_over(out, press, out_copy, press_copy, out_v, press_v, sem_in, sem_out):
    chunks = [(r.at[i], v.at[i], c.at[i]) for r, v, c in ((out, out_v, out_copy),) for i in range(3)]
    chunks.append((press, press_v, press_copy))
    get = [pltpu.make_async_copy(c[0], c[1], sem_in.at[k]) for k, c in enumerate(chunks)]
    put = [pltpu.make_async_copy(c[1], c[2], sem_out.at[k]) for k, c in enumerate(chunks)]
    for c in get:
        c.start()
    for g, p in zip(get, put):
        g.wait()
        p.start()
    for c in put:
        c.wait()


def solution(mesh):
    ngx, ngy = mesh.shape["gx"], mesh.shape["gy"]

    def per_device(
        disp_start, load, modulus, element_matrix, precond, approach, contact, owner, slot, influence
    ):
        vm = lambda shape, dtype=F32: pltpu.VMEM(shape, dtype)
        dma = lambda n: pltpu.SemaphoreType.DMA((n,))
        anywhere = pl.BlockSpec(memory_space=pltpu.HBM)
        results = pl.pallas_call(
            functools.partial(kernel, ngx, ngy),
            out_shape=(
                jax.ShapeDtypeStruct((3, 8, 32, 256), F32),
                jax.ShapeDtypeStruct((8, 256), F32),
            ),
            in_specs=[anywhere] * 13,
            out_specs=(anywhere, anywhere),
            scratch_shapes=[
                vm((3, 10, 32, 256)), vm((3, 10, 32, 256)),
                vm((3, 8, 32, 256)), vm((3, 8, 32, 256)), vm((9, 8, 32, 256)),
                vm((9, 32, 256)), vm((9, 32, 256)), vm((9, 32, 256)),
                vm((2, 10, COLS, 256), BF16), vm((2, 10, COLS, 256), BF16),
                vm((ROWS, 2 * COLS), BF16), vm((ROWS, 2 * COLS), BF16),
                vm((2, 2 * COLS, 128), BF16), vm((2, 2 * COLS, 128), BF16),
                vm((32, 128)), vm((32, 128)), vm((2, 3, 16, 128)),
                vm((3, 8, 32, 256)), vm((8, 256)),
                vm((24, 24)), vm((ROWS, 24), BF16), vm((24, 4 * COLS), BF16), vm((ROWS, 4 * COLS), BF16),
                vm((1, 8)), vm((4, 8), jnp.int32), vm((4, 8), jnp.int32), vm((4, 8), jnp.int32),
                vm((32, TW, TW)), vm((16, 128, 128), BF16), vm((16, 128, 128), BF16),
                vm((2, 8, 128)), vm((1, 8, 128)), vm((1, 8, 128)), vm((1, 8, 128)),
                vm((3, 2, 8, 128)), vm((3, 1, 8, 128)), vm((3, 1, 8, 128)), vm((3, 1, 8, 128)),
                vm((16, TW, 128)), vm((16, TW, 128)),
                dma(18), dma(17), dma(17), dma(16), dma(16),
            ],
            compiler_params=pltpu.CompilerParams(
                collective_id=0, has_side_effects=True, vmem_limit_bytes=60 * 1024 * 1024
            ),
        )(
            disp_start, load, modulus, element_matrix, precond, approach.reshape(1, 8),
            contact.T, owner.T, slot.T, influence.reshape(32, TW, TW), *tables(),
        )
        return pl.pallas_call(
            hand_over,
            out_shape=tuple(jax.ShapeDtypeStruct(r.shape, r.dtype) for r in results),
            in_specs=[anywhere] * 2,
            out_specs=(anywhere, anywhere),
            scratch_shapes=[vm((3, 8, 32, 256)), vm((8, 256)), dma(4), dma(4)],
            compiler_params=pltpu.CompilerParams(vmem_limit_bytes=60 * 1024 * 1024),
        )(*results)

    return jax.shard_map(
        per_device,
        mesh=mesh,
        in_specs=(
            P(None, "gx", None, "gy"),
            P(None, "gx", None, "gy"),
            P("gx", None, "gy"),
            P(),
            P(None, "gx", None, "gy"),
            P("gx"),
            P("gx", "gy"),
            P("gx", "gy"),
            P("gx", "gy"),
            P("gx", "gy", None, None, None, None),
        ),
        out_specs=(P(None, "gx", None, "gy"), P("gx", "gy")),
        check_vma=False,
    )
```
